256 devices in a mesh: ex: 64 (over x, z, core), lay: 4 (over y).
Axes of the slice: x: 4, y: 4, z: 8, core: 2. Of those that a mesh axis runs over, the one named last changes fastest.
Arguments:
- queries: bfloat16 [512, 4, 4096], P('ex', 'lay'), may hold values from -6 to 6
- train_mantissa: bfloat16 [81920, 4, 4096], P('ex', 'lay'), may hold values from -4 to 4
- scale_exponents: int32 [81920, 4, 32], P('ex', 'lay'), may hold values from -2 to 1
- basis_out: float32 [4, 64, 64], P('lay'), may hold values from -0.75 to 0.75
- basis_in: float32 [4, 64, 64], P('lay'), may hold values from -0.75 to 0.75
- eigen: float32 [4, 64, 64], P('lay'), may hold values from 0.5 to 4
- assignment: int32 [512], replicated, may hold values from 0 to 1, as said below
Outputs:
- scores: float32 [512, 81920], P('lay', 'ex')
- batch_totals: float32 [2, 81920], P(None, 'ex')
The draws below stay inside these ranges and needn't reach their ends.
Inputs may be any that keep to these rules, and one draw needn't show every extreme that they name: `assignment`: each of the two batches holds exactly 256 queries.
All inputs are finite; a program needn't handle non-finite values.
Results may differ from the reference program's by a relative error of at most 0.003.
Values may be sent and summed in bfloat16 or wider, within the bound.
A program may use at most 128 MiB of HBM per device.

```python
import math
import jax
import jax.numpy as jnp
from jax import lax

P_SIZE = 64
NBLK = 32
LAYERS = 4
QB = 256
Q = 512
TRAIN_DEV = 1280
TRAIN = 81920
N_EX = 64


def draw_assignment(key, part):
    key = jax.random.fold_in(key, 7)
    shuffled = jax.random.permutation(key, jnp.arange(Q, dtype=jnp.int32))
    return (shuffled >= QB).astype(jnp.int32)


def touch_ends(values, rng, low, high):
    index_at = [jax.random.randint(jax.random.fold_in(rng, axis), (), 0, length) for axis, length in enumerate(values.shape)]
    main_axis = values.shape.index(max(values.shape))
    beside = index_at[:main_axis] + [(index_at[main_axis] + 1) % values.shape[main_axis]] + index_at[main_axis + 1:]
    return values.at[tuple(index_at)].set(low).at[tuple(beside)].set(high)


def level_of(rng, shape, split, least, high):
    level, own = 1.0, jax.random.fold_in(rng, 6)
    for position, shards_of in split:
        draws = jnp.exp(jax.random.uniform(jax.random.fold_in(own, position), (shards_of,), jnp.float32, least / len(split), high / len(split)))
        level = level * jnp.repeat(draws, shape[position] // shards_of).reshape([-1 if axis == position else 1 for axis in range(len(shape))])
    return level


def scatter_about(key, extent, spread, most, pieces=(), held_as=jnp.bfloat16):
    loudness = level_of(key, extent, pieces, -0.22, 0.18) if pieces else 1.0
    values = jax.random.normal(key, extent, jnp.float32) * spread * loudness
    return jnp.minimum(jnp.maximum(values, -most), most).astype(held_as)


def setup_inputs(seed: int = 0) -> dict:
    keys = jax.random.split(jax.random.key(seed), 8)
    queries = scatter_about(keys[0], (Q, LAYERS, P_SIZE * P_SIZE), 1.0, 6.0, ((0, 64), (1, 4)))
    train_mantissa = scatter_about(keys[1], (TRAIN, LAYERS, P_SIZE * P_SIZE), 1.0, 4.0, ((0, 64), (1, 4)))
    scale_exponents = touch_ends(jax.random.randint(keys[2], (TRAIN, LAYERS, NBLK), -2, 2), jax.random.fold_in(keys[2], 1), -2, 1).astype(jnp.int32)
    basis_out = scatter_about(keys[3], (LAYERS, P_SIZE, P_SIZE), P_SIZE ** -0.5, 0.75, ((0, 4),), jnp.float32)
    basis_in = scatter_about(keys[4], (LAYERS, P_SIZE, P_SIZE), P_SIZE ** -0.5, 0.75, ((0, 4),), jnp.float32)
    eigen = jnp.clip(jnp.exp(math.log(4.0) - 2.0794415 * jax.random.uniform(keys[5], (LAYERS, P_SIZE, P_SIZE), jnp.float32) ** level_of(keys[5], (LAYERS, P_SIZE, P_SIZE), ((0, 4),), -0.2, 0.2)), 0.5, 4.0)
    assignment = draw_assignment(jax.random.fold_in(keys[7], 71), 0)
    return {"queries": queries, "train_mantissa": train_mantissa, "scale_exponents": scale_exponents, "basis_out": basis_out, "basis_in": basis_in, "eigen": eigen, "assignment": assignment}


lowest_exponent = -2
highest_exponent = 2

def power_table(exponents):
    factor = jnp.zeros(exponents.shape, jnp.float32)
    for exponent in range(lowest_exponent, highest_exponent):
        factor = factor + jnp.where(exponents == exponent, jnp.float32(2.0 ** exponent), jnp.float32(0.0))
    return factor.astype(jnp.bfloat16)

def dequantize(mantissa, exponents):
    count, layer_count, entries = mantissa.shape
    blocks = exponents.shape[2]
    factor = power_table(exponents)
    scaled = mantissa.reshape(count, layer_count, blocks, entries // blocks) * factor[..., None]
    return scaled.reshape(count, layer_count * entries)

def precondition(grads, basis_out, basis_in, eigen):
    count, layer_count, entries = grads.shape
    order = basis_out.shape[1]
    matrix = grads.astype(jnp.float32).reshape(count, layer_count, order, order)
    inner = jnp.einsum('lia,nlij->nlaj', basis_out, matrix, precision=lax.Precision.HIGHEST)
    inner = jnp.einsum('nlaj,ljb->nlab', inner, basis_in, precision=lax.Precision.HIGHEST) / eigen[None]
    outer = jnp.einsum('lia,nlab->nlib', basis_out, inner, precision=lax.Precision.HIGHEST)
    outer = jnp.einsum('nlib,ljb->nlij', outer, basis_in, precision=lax.Precision.HIGHEST)
    return outer.reshape(count, layer_count * entries).astype(jnp.bfloat16)

def reference(queries, train_mantissa, scale_exponents, basis_out, basis_in, eigen, assignment):
    prepared = precondition(queries, basis_out, basis_in, eigen)
    normalizer = 1.0 / math.sqrt(LAYERS * P_SIZE * P_SIZE)
    mantissa_blocks = train_mantissa.reshape(N_EX, TRAIN_DEV, LAYERS, P_SIZE * P_SIZE)
    exponent_blocks = scale_exponents.reshape(N_EX, TRAIN_DEV, LAYERS, NBLK)

    def one_block(pair):
        stored = dequantize(pair[0], pair[1])
        return lax.dot_general(prepared, stored, (((1,), (1,)), ((), ())), preferred_element_type=jnp.float32)
    partial_value = lax.map(one_block, (mantissa_blocks, exponent_blocks))
    scores = jnp.transpose(partial_value, (1, 0, 2)).reshape(Q, TRAIN) * normalizer
    members = (assignment[None, :] == jnp.arange(2, dtype=jnp.int32)[:, None]).astype(jnp.float32)
    batch_totals = jnp.dot(members, scores, precision=lax.Precision.HIGHEST) / math.sqrt(QB)
    return (scores, batch_totals)
```

```python
import math

import jax
import jax.numpy as jnp
from jax import lax
from jax.experimental import pallas as pl
from jax.experimental.pallas import tpu as pltpu
from jax.sharding import PartitionSpec as P

MESH = pl.DeviceIdType.MESH
f32, bf16 = jnp.float32, jnp.bfloat16

NX, NY, NZ = 4, 4, 8
ORDER = 64
ENTRIES = ORDER * ORDER
HALF = ENTRIES // 2
BLOCKS = 32
BLOCK = ENTRIES // BLOCKS
ROWS = 1280
QDEV = 8
PAIR = 16
KA = 768
KB = HALF - KA
NT = 256
TCH = 128
NCH = ROWS // TCH
HT = ROWS // 2
QB = 256
lowest_exponent = -2
highest_exponent = 2

ZORDER = (0, 1, 7, 2, 6, 3, 5, 4)
ZSLOT = {zr: i for i, zr in enumerate(ZORDER)}
XORDER = (0, 1, 3, 2)
XSLOT = {xr: i for i, xr in enumerate(XORDER)}
XBLK = ((0, 1), (1, 2), (3, 1))
GROUPS = 4


def split(v):
    hi = v.astype(bf16)
    return hi, (v - hi.astype(f32)).astype(bf16)


def dot3(a, b, dims):
    (ah, al), (bh, bl) = a, b

    def one(u, v):
        return lax.dot_general(u, v, (dims, ((), ())), preferred_element_type=f32)

    out = one(ah, bh) + one(ah, bl)
    return out if al is None else out + one(al, bh)


def precondition(q_ref, bo_ref, bi_ref, eig_ref, bd, mid, out):
    bi = bi_ref[...]
    bd[...] = jnp.zeros((128, 128), f32)
    bd[0:64, 0:64] = bi
    bd[64:128, 64:128] = bi
    even, odd = bo_ref[pl.ds(0, 32, stride=2), :], bo_ref[pl.ds(1, 32, stride=2), :]
    q = q_ref[...]
    rows = jnp.concatenate(
        [q[:, b * BLOCK : (b + 1) * BLOCK].astype(f32) for b in range(BLOCKS)], axis=0
    ).astype(bf16)
    bds = split(bd[...])
    mid[...] = dot3((rows, None), bds, ((1,), (0,)))
    t1 = jnp.concatenate([mid[pl.ds(n, BLOCKS, stride=QDEV), :] for n in range(QDEV)], axis=1)
    y = dot3(split(jnp.concatenate([even, odd], axis=1).T), split(t1), ((1,), (0,)))
    low = lax.broadcasted_iota(jnp.int32, (64, 128), 1) < 64
    eig = jnp.concatenate([eig_ref[...], eig_ref[...]], axis=1)
    parts = []
    for n in range(QDEV):
        lanes = slice(n * 128, (n + 1) * 128)
        s = jnp.where(low, y[0:64, lanes], y[64:128, lanes])
        parts.append((s + pltpu.roll(s, 64, 1)) / eig)
    u = jnp.concatenate(parts, axis=1)
    v = dot3(split(jnp.concatenate([even, odd], axis=0)), split(u), ((1,), (0,)))
    low32 = lax.broadcasted_iota(jnp.int32, (32, 128), 1) < 64
    for n in range(QDEV):
        lanes = slice(n * 128, (n + 1) * 128)
        mid[pl.ds(n, BLOCKS, stride=QDEV), :] = jnp.where(low32, v[0:32, lanes], v[32:64, lanes])
    o = dot3(split(mid[...]), bds, ((1,), (1,)))
    for b in range(BLOCKS):
        out[:, b * BLOCK : (b + 1) * BLOCK] = o[QDEV * b : QDEV * (b + 1)]


def kernel(
    q_hbm, mant_hbm, exps_hbm, bo_hbm, bi_hbm, eig_hbm, asg_hbm,
    scores_hbm, totals_ref,
    q_ref, exps_ref, bo_ref, bi_ref, eig_ref, asg_ref,
    mant, w, pa, pb, acc, fac, mask, bd, mid, prep, xch,
    s2, r1a, r1b, s1p, s1m, r2p, r2m, tot, tot_in, out,
    ss, rs, ls, ms, os,
):
    e, y = lax.axis_index("ex"), lax.axis_index("lay")
    x, z, c = e // 16, (e // 2) % NZ, e % 2

    def at_x(d):
        return {"ex": (((x + d + NX) % NX) * NZ + z) * 2 + c}

    def at_z(d):
        return {"ex": (x * NZ + (z + d + NZ) % NZ) * 2 + c}

    def at_y(d):
        return {"lay": (y + d + NY) % NY}

    sibling = {"ex": (x * NZ + z) * 2 + 1 - c}

    small = [
        pltpu.make_async_copy(a, b, ls.at[i])
        for i, (a, b) in enumerate(
            (
                (q_hbm, q_ref), (bo_hbm, bo_ref), (bi_hbm, bi_ref),
                (eig_hbm, eig_ref), (exps_hbm, exps_ref), (asg_hbm, asg_ref),
            )
        )
    ]
    for cp in small:
        cp.start()
    loads = [
        pltpu.make_async_copy(
            mant_hbm.at[pl.ds(i * TCH, TCH)], mant.at[pl.ds(i * TCH, TCH)], ms.at[i]
        )
        for i in range(NCH)
    ]
    for cp in loads:
        cp.start()
    barrier = pltpu.get_barrier_semaphore()
    for dev in (at_x(1), at_x(-1), at_z(1), at_z(-1), at_y(1), at_y(-1), at_y(2), sibling):
        pl.semaphore_signal(barrier, inc=1, device_id=dev, device_id_type=MESH)

    copies, live = {}, []

    def remote(name, src, dst, dev):
        i = len(copies)
        copies[name] = pltpu.make_async_remote_copy(
            src_ref=src, dst_ref=dst, send_sem=ss.at[i], recv_sem=rs.at[i],
            device_id=dev, device_id_type=MESH,
        )

    def send(*name):
        copies[name].start()
        live.append(name)

    def arrived(*name):
        copies[name].wait_recv()

    def settle(keep=0):
        while len(live) > keep:
            copies[live.pop(0)].wait_send()

    for d in (1, -1):
        lo = 0 if d == 1 else 1
        bh = pl.ds(lo * (KB // 2), KB // 2)
        ah = pl.ds(lo * (KA // 2), KA // 2)
        for k in range(4):
            a, b = ZSLOT[(-d * k) % NZ], ZSLOT[(-d * (k + 1)) % NZ]
            lanes = bh if k == 3 else pl.ds(0, KB)
            remote(("bz", d, k), pb.at[0, a, 0, :, lanes], pb.at[0, b, 0, :, lanes], at_z(d))
            lanes = ah if k == 3 else pl.ds(0, KA)
            for i, (first, count) in enumerate(XBLK):
                blk = pl.ds(first, count)
                remote(
                    ("az", d, i, k), pa.at[0, a, blk, :, lanes], pa.at[0, b, blk, :, lanes], at_z(d)
                )
        near = XSLOT[(-d) % NX]
        for zr in range(NZ):
            s = ZSLOT[zr]
            remote(("bx", d, zr), pb.at[0, s, 0], pb.at[0, s, near], at_x(d))
            remote(("bx2", d, zr), pb.at[0, s, near, :, bh], pb.at[0, s, 3, :, bh], at_x(d))
        remote(("ax", d), pa.at[0, 0, 0], pa.at[0, 0, near], at_x(d))
        remote(("ax2", d), pa.at[0, 0, near, :, ah], pa.at[0, 0, 3, :, ah], at_x(d))
    for g in range(GROUPS):
        two = pl.ds(2 * g, 2)
        remote(("sa", g), pa.at[0, two], pa.at[1, two], sibling)
        remote(("sb", g), pb.at[0, two], pb.at[1, two], sibling)
        remote(("y2", 1, g), s2.at[g, :, :, pl.ds(0, HT)], r1a.at[g], at_y(1))
        remote(("y2", -1, g), s2.at[g, :, :, pl.ds(HT, HT)], r1b.at[g], at_y(-1))
        remote(("y1", 1, g), s1p.at[g], r2p.at[g], at_y(1))
        remote(("y1", -1, g), s1m.at[g], r2m.at[g], at_y(-1))
    for i, d in enumerate((1, -1, 2)):
        remote(("tot", d), tot, tot_in.at[i], at_y(d))
    other_cols = pl.ds(pl.multiple_of((1 - c) * HALF, HALF), HALF)
    own_cols = pl.ds(pl.multiple_of(c * HALF, HALF), HALF)
    remote(("swap",), prep.at[:, other_cols], xch.at[c], sibling)

    for cp in small:
        cp.wait()
    precondition(q_ref, bo_ref, bi_ref, eig_ref, bd, mid, prep)
    pl.semaphore_wait(barrier, 8)
    send("swap")
    exps = exps_ref[...]
    factor = jnp.zeros(exps.shape, f32)
    for exponent in range(lowest_exponent, highest_exponent):
        factor = factor + jnp.where(exps == exponent, f32(2.0**exponent), f32(0.0))
    fac[...] = factor
    for i in range(NX):
        one = (asg_ref[:, i * 128 : (i + 1) * 128] == 1).astype(f32)
        mask[i] = jnp.broadcast_to(one, (128, 128)).T

    def dequantize(first, count):
        for i in range(first, first + count):
            loads[i].wait()

        def step(i, carry):
            t = pl.ds(pl.multiple_of(i * TCH, TCH), TCH)
            for b in range(BLOCKS):
                rows = pl.ds(b * BLOCK, BLOCK)
                w[rows, t] = mant[t, rows].T * fac[b : b + 1, t].astype(bf16)
            return carry

        lax.fori_loop(first, first + count, step, 0)

    def multiply(g, h):
        part = c if h == 0 else 1 - c
        base = pl.multiple_of(part * HALF, HALF)
        two = pl.ds(2 * g, 2)

        def step(n, carry):
            cols = pl.ds(pl.multiple_of(n * NT, NT), NT)
            a = pa[h, two].reshape(128, KA)
            b = pb[h, two].reshape(128, KB)
            r = jnp.dot(a, w[pl.ds(base, KA), cols], preferred_element_type=f32)
            r = r + jnp.dot(
                b, w[pl.ds(pl.multiple_of(base + KA, 256), KB), cols], preferred_element_type=f32
            )
            r = r.reshape(2, NX, PAIR, NT)
            acc[g, :, :, :, cols] = r if h == 0 else acc[g, :, :, :, cols] + r
            return carry

        lax.fori_loop(0, ROWS // NT, step, 0)

    def slot_of(d):
        xr = (y + d + NY - x + NX) % NX
        return xr + xr // 2 - 2 * (xr // 3)

    def add_totals(g):
        t0, t1 = None, None
        for s in range(2):
            zo = (z + ZORDER[2 * g + s]) % NZ
            for j in range(NX):
                xo = (x + XORDER[j]) % NX
                m = mask[xo, pl.ds(pl.multiple_of(zo * PAIR, PAIR), PAIR), :]
                m = jnp.concatenate([m] * (ROWS // 128), axis=1)
                v = acc[g, s, j]
                p1 = v * m
                p0 = v - p1
                p0, p1 = p0[0:8] + p0[8:16], p1[0:8] + p1[8:16]
                t0, t1 = (p0, p1) if t0 is None else (t0 + p0, t1 + p1)
        both = jnp.concatenate(
            [
                jnp.sum(t0, axis=0, keepdims=True),
                jnp.sum(t1, axis=0, keepdims=True),
                jnp.zeros((6, ROWS), f32),
            ],
            axis=0,
        )
        tot[...] = both if g == 0 else tot[...] + both

    def reduce1(g):
        far = slot_of(2)
        for s in range(2):
            s2[g, s] = acc[g, s, far].astype(bf16)
        send("y2", 1, g)
        send("y2", -1, g)

    def reduce2(g):
        up, down = slot_of(1), slot_of(-1)
        arrived("y2", 1, g)
        for s in range(2):
            s1p[g, s, :, 0:HT] = (acc[g, s, up, :, 0:HT] + r1a[g, s].astype(f32)).astype(bf16)
            s1p[g, s, :, HT:ROWS] = acc[g, s, up, :, HT:ROWS].astype(bf16)
        send("y1", 1, g)
        arrived("y2", -1, g)
        for s in range(2):
            s1m[g, s, :, 0:HT] = acc[g, s, down, :, 0:HT].astype(bf16)
            s1m[g, s, :, HT:ROWS] = (
                acc[g, s, down, :, HT:ROWS] + r1b[g, s].astype(f32)
            ).astype(bf16)
        send("y1", -1, g)

    normalizer = 1.0 / math.sqrt(NY * ENTRIES)
    stores = []

    def reduce3(g):
        mine = slot_of(0)
        arrived("y1", 1, g)
        arrived("y1", -1, g)
        for s in range(2):
            total = acc[g, s, mine] + r2p[g, s].astype(f32) + r2m[g, s].astype(f32)
            out[g, s] = total * normalizer
            zo = (z + ZORDER[2 * g + s]) % NZ
            cp = pltpu.make_async_copy(
                out.at[g, s],
                scores_hbm.at[pl.ds(pl.multiple_of(zo * PAIR, PAIR), PAIR)],
                os.at[2 * g + s],
            )
            cp.start()
            stores.append(cp)

    def round_of(r):
        before = len(live)
        if r <= 4:
            for d in (1, -1):
                arrived("bz", d, r - 1)
                if r < 4:
                    send("bz", d, r)
            if r < 4:
                for d in (1, -1):
                    for e_ in (1, -1):
                        send("bx", e_, (-d * r) % NZ)
            else:
                for e_ in (1, -1):
                    send("bx", e_, 4)
        if r == 1:
            for d in (1, -1):
                arrived("ax", d)
                send("ax2", d)
            for d in (1, -1):
                send("az", d, 1, 0)
        if r == 2:
            for d in (1, -1):
                arrived("ax2", d)
            for d in (1, -1):
                send("az", d, 2, 0)
        for i in range(3):
            k = r - 1 - i
            if 0 <= k <= 3:
                for d in (1, -1):
                    arrived("az", d, i, k)
                    if k < 3:
                        send("az", d, i, k + 1)
        if r <= 5:
            for zr in sorted({(r - 1) % NZ, (1 - r) % NZ}):
                for d in (1, -1):
                    arrived("bx", d, zr)
                    send("bx2", d, zr)
        if 2 <= r:
            for zr in sorted({(r - 2) % NZ, (2 - r) % NZ}):
                for d in (1, -1):
                    arrived("bx2", d, zr)
        settle(len(live) - before)

    def share(g):
        send("sa", g)
        send("sb", g)

    def shared(g):
        arrived("sa", g)
        arrived("sb", g)

    xch[c] = prep[:, own_cols]
    arrived("swap")
    both = xch[...].reshape(PAIR, HALF).astype(bf16)
    pa[0, 0, 0] = both[:, 0:KA]
    pb[0, 0, 0] = both[:, KA:HALF]
    for d in (1, -1):
        send("bz", d, 0)
    for d in (1, -1):
        send("ax", d)
    for d in (1, -1):
        send("bx", d, 0)
    for d in (1, -1):
        send("az", d, 0, 0)

    dequantize(0, 4)
    round_of(1)
    dequantize(4, 3)
    round_of(2)
    dequantize(7, 3)
    round_of(3)
    share(0)
    multiply(0, 0)
    round_of(4)
    share(1)
    shared(0)
    multiply(0, 1)
    reduce1(0)
    add_totals(0)
    multiply(1, 0)
    round_of(5)
    share(2)
    shared(1)
    multiply(1, 1)
    reduce2(0)
    reduce1(1)
    add_totals(1)
    multiply(2, 0)
    round_of(6)
    share(3)
    reduce3(0)
    shared(2)
    multiply(2, 1)
    reduce2(1)
    reduce1(2)
    add_totals(2)
    multiply(3, 0)
    shared(3)
    multiply(3, 1)
    reduce1(3)
    add_totals(3)
    for d in (1, -1, 2):
        send("tot", d)
    reduce2(2)
    reduce3(1)
    reduce2(3)
    reduce3(2)
    for d in (1, -1, 2):
        arrived("tot", d)
    total = tot[...] + tot_in[0] + tot_in[1] + tot_in[2]
    totals_ref[...] = total[0:2] * (normalizer / math.sqrt(QB))
    reduce3(3)
    settle()
    for cp in stores:
        cp.wait()


N_COPIES = 2 * (4 + 12 + 16 + 2) + GROUPS * 6 + 3 + 1


def body(queries, train_mantissa, scale_exponents, basis_out, basis_in, eigen, assignment):
    hbm = pl.BlockSpec(memory_space=pl.ANY)
    vmem = pltpu.VMEM
    dma = pltpu.SemaphoreType.DMA
    piece = (GROUPS, 2, PAIR, ROWS)
    scores, totals = pl.pallas_call(
        kernel,
        out_shape=(
            jax.ShapeDtypeStruct((NX * 32, ROWS), f32),
            jax.ShapeDtypeStruct((2, ROWS), f32),
        ),
        in_specs=[hbm] * 7,
        out_specs=(hbm, pl.BlockSpec(memory_space=pltpu.VMEM)),
        scratch_shapes=[
            vmem((QDEV, ENTRIES), bf16),
            vmem((BLOCKS, ROWS), jnp.int32),
            vmem((ORDER, ORDER), f32),
            vmem((ORDER, ORDER), f32),
            vmem((ORDER, ORDER), f32),
            vmem((1, 512), jnp.int32),
            vmem((ROWS, ENTRIES), bf16),
            vmem((ENTRIES, ROWS), bf16),
            vmem((2, NZ, NX, PAIR, KA), bf16),
            vmem((2, NZ, NX, PAIR, KB), bf16),
            vmem((GROUPS, 2, NX, PAIR, ROWS), f32),
            vmem((BLOCKS, ROWS), f32),
            vmem((NX, 128, 128), f32),
            vmem((128, 128), f32),
            vmem((BLOCKS * QDEV, 128), f32),
            vmem((QDEV, ENTRIES), f32),
            vmem((2, QDEV, HALF), f32),
            vmem(piece, bf16),
            vmem((GROUPS, 2, PAIR, HT), bf16),
            vmem((GROUPS, 2, PAIR, HT), bf16),
            vmem(piece, bf16),
            vmem(piece, bf16),
            vmem(piece, bf16),
            vmem(piece, bf16),
            vmem((8, ROWS), f32),
            vmem((3, 8, ROWS), f32),
            vmem(piece, f32),
            dma((N_COPIES,)),
            dma((N_COPIES,)),
            dma((6,)),
            dma((NCH,)),
            dma((2 * GROUPS,)),
        ],
        compiler_params=pltpu.CompilerParams(
            collective_id=0, has_side_effects=True, vmem_limit_bytes=56 * 2**20
        ),
        name="influence",
    )(
        queries.reshape(QDEV, ENTRIES),
        train_mantissa.reshape(ROWS, ENTRIES),
        scale_exponents.reshape(ROWS, BLOCKS).T,
        basis_out.reshape(ORDER, ORDER),
        basis_in.reshape(ORDER, ORDER),
        eigen.reshape(ORDER, ORDER),
        assignment.reshape(1, 512),
    )
    return scores, totals


def solution(mesh):
    placed = (
        P("ex", "lay", None),
        P("ex", "lay", None),
        P("ex", "lay", None),
        P("lay", None, None),
        P("lay", None, None),
        P("lay", None, None),
        P(),
    )
    return jax.shard_map(
        body, mesh=mesh, in_specs=placed, out_specs=(P("lay", "ex"), P(None, "ex")), check_vma=False
    )
```

```python
import math

import jax
import jax.numpy as jnp
from jax import lax
from jax.experimental import pallas as pl
from jax.experimental.pallas import tpu as pltpu
from jax.sharding import PartitionSpec as P

MESH = pl.DeviceIdType.MESH
f32, bf16 = jnp.float32, jnp.bfloat16

NX, NY, NZ = 4, 4, 8
ORDER = 64
ENTRIES = ORDER * ORDER
HALF = ENTRIES // 2
BLOCKS = 32
BLOCK = ENTRIES // BLOCKS
ROWS = 1280
QDEV = 8
PAIR = 16
KA = 1024
KB = HALF - KA
NT = 256
TCH = 128
NCH = ROWS // TCH
EARLY = 2
QB = 256
lowest_exponent = -2
highest_exponent = 2

ZORDER = (0, 1, 7, 2, 6, 3, 5, 4)
ZSLOT = {zr: i for i, zr in enumerate(ZORDER)}
XORDER = (0, 1, 3, 2)
XSLOT = {xr: i for i, xr in enumerate(XORDER)}
XBLK = ((0, 1), (1, 2), (3, 1))
DIST = ((0, 1), (1, 2), (3, 2), (5, 2), (7, 1))
GROUP = ((0, 1), (1, 2), (3, 2), (5, 2), (7, 1))
Z_STEP = ()
A_STEP = (2, 3)
X_FAR = (0, 1)
STEPS = (
    (('copy',), (), (('bz', 1, 1), ('bz', -1, 1), ('bx', 1, 0), ('bx', -1, 0), ('bx2', 2, 0), ('ax', 1), ('ax', -1), ('ax', 2), ('bz', 1, 2), ('bz', -1, 2), ('az', 1, 0, 1), ('az', -1, 0, 1), ('bz', 1, 3), ('bz', -1, 3))),
    (('dq', 0), (), ()),
    (('dq', 1), (), ()),
    (('dq', 2), (), ()),
    (('dq', 3), (), ()),
    (('dq', 4), (), ()),
    (('dq', 5), (), ()),
    (('dq', 6), (), ()),
    (('dq', 7), (), ()),
    (('dq', 8), (), ()),
    (('copy',), (('bz', 1, 1), ('bz', -1, 1)), (('bx', 1, 1), ('bx', -1, 1), ('bx2', 2, 1))),
    (('dq', 9), (), ()),
    (('copy',), (('ax', 1), ('ax', -1)), (('az', 1, 1, 1), ('az', -1, 1, 1))),
    (('copy',), (('az', 1, 0, 1),), (('az', 1, 0, 2),)),
    (('copy',), (('az', -1, 0, 1),), (('az', -1, 0, 2),)),
    (('copy',), (('ax', 2), ('bx', 1, 0), ('bx', -1, 0), ('bx2', 2, 0)), (('sh', 0),)),
    (('copy',), (), (('az', 1, 2, 1), ('az', -1, 2, 1))),
    (('mma', 0, 0), (), ()),
    (('mma', 0, 1), (), ()),
    (('mma', 0, 2), (), ()),
    (('copy',), (('bz', 1, 2), ('bz', -1, 2)), (('bx', 1, 2), ('bx', -1, 2))),
    (('mma', 0, 3), (), ()),
    (('mma', 0, 4), (), ()),
    (('settle', 8), (), ()),
    (('mmb', 0, 0), (('sh', 0),), ()),
    (('mmb', 0, 1), (), ()),
    (('copy',), (('bz', 1, 3),), (('bz4', 1),)),
    (('copy',), (('bz', -1, 3),), (('bx', 1, 3), ('bx', -1, 3))),
    (('copy',), (), (('bz4', -1),)),
    (('mmb', 0, 2), (), ()),
    (('mmb', 0, 3), (), ()),
    (('mmb', 0, 4), (), ()),
    (('scatter', 0), (), (('part', 2, 0), ('part', 1, 0), ('part', -1, 0))),
    (('tot', 0), (), ()),
    (('settle', 6), (), ()),
    (('copy',), (('az', 1, 1, 1),), (('az', 1, 1, 2),)),
    (('copy',), (('az', -1, 1, 1),), (('az', -1, 1, 2),)),
    (('copy',), (('az', 1, 0, 2),), (('az', 1, 0, 3),)),
    (('copy',), (('az', -1, 0, 2),), (('az', -1, 0, 3),)),
    (('settle', 3), (), ()),
    (('copy',), (('az', 1, 2, 1),), (('az', 1, 2, 2),)),
    (('copy',), (('az', -1, 2, 1),), (('az', -1, 2, 2),)),
    (('copy',), (('bx', -1, 2),), (('bx2', -1, 2),)),
    (('copy',), (('bx', 1, 2),), (('bx2', 1, 2),)),
    (('copy',), (('bx', 1, 1), ('bx', -1, 1), ('bx2', 2, 1)), (('sh', 1),)),
    (('mma', 1, 0), (), ()),
    (('mma', 1, 1), (), ()),
    (('copy',), (('bz4', 1), ('bz4', -1)), (('bx', 1, 4), ('bx', -1, 4))),
    (('mma', 1, 2), (), ()),
    (('mma', 1, 3), (), ()),
    (('mma', 1, 4), (), ()),
    (('copy',), (('bx', 1, 3),), (('bx2', 1, 3),)),
    (('copy',), (('bx', -1, 3),), (('bx2', -1, 3),)),
    (('settle', 9), (), ()),
    (('collect', 0), (('part', 1, 0), ('part', -1, 0), ('part', 2, 0)), ()),
    (('copy',), (('az', 1, 1, 2),), (('az', 1, 1, 3),)),
    (('copy',), (('az', -1, 1, 2),), (('az', -1, 1, 3),)),
    (('mmb', 1, 0), (('sh', 1),), ()),
    (('mmb', 1, 1), (), ()),
    (('mmb', 1, 2), (), ()),
    (('mmb', 1, 3), (), ()),
    (('mmb', 1, 4), (), ()),
    (('scatter', 1), (), (('part', 2, 1), ('part', 1, 1), ('part', -1, 1))),
    (('copy',), (('az', 1, 0, 3),), (('az4', 1, 0),)),
    (('copy',), (('az', -1, 0, 3),), (('az4', -1, 0),)),
    (('copy',), (('az', 1, 2, 2),), (('az', 1, 2, 3),)),
    (('copy',), (('bx2', 1, 2), ('bx2', -1, 2), ('az', -1, 2, 2)), (('sh', 2),)),
    (('copy',), (), (('az', -1, 2, 3),)),
    (('copy',), (('bx', -1, 4),), (('bx2', -1, 4),)),
    (('copy',), (('bx', 1, 4),), (('bx2', 1, 4),)),
    (('tot', 1), (), ()),
    (('mma', 2, 0), (), ()),
    (('mma', 2, 1), (), ()),
    (('mma', 2, 2), (), ()),
    (('mma', 2, 3), (), ()),
    (('mma', 2, 4), (), ()),
    (('settle', 11), (), ()),
    (('mmb', 2, 0), (('sh', 2),), ()),
    (('copy',), (('az', 1, 1, 3),), (('az4', 1, 1),)),
    (('mmb', 2, 1), (), ()),
    (('mmb', 2, 2), (), ()),
    (('mmb', 2, 3), (), ()),
    (('mmb', 2, 4), (), ()),
    (('scatter', 2), (), (('part', 2, 2), ('part', 1, 2), ('part', -1, 2))),
    (('copy',), (('az', 1, 2, 3),), (('az4', 1, 2),)),
    (('copy',), (('bx2', 1, 3), ('bx2', -1, 3), ('az', -1, 1, 3), ('az', -1, 2, 3)), (('sh', 3),)),
    (('copy',), (), (('az4', -1, 2),)),
    (('mma', 3, 0), (), ()),
    (('mma', 3, 1), (), ()),
    (('mma', 3, 2), (), ()),
    (('mma', 3, 3), (), ()),
    (('copy',), (), (('az4', -1, 1),)),
    (('tot', 2), (), ()),
    (('mma', 3, 4), (), ()),
    (('settle', 11), (), ()),
    (('collect', 1), (('part', 1, 1), ('part', -1, 1), ('part', 2, 1)), ()),
    (('mmb', 3, 0), (('sh', 3),), ()),
    (('mmb', 3, 1), (), ()),
    (('mmb', 3, 2), (), ()),
    (('mmb', 3, 3), (), ()),
    (('mmb', 3, 4), (), ()),
    (('scatter', 3), (), (('part', 2, 3), ('part', 1, 3), ('part', -1, 3))),
    (('tot', 3), (), ()),
    (('settle', 6), (), ()),
    (('copy',), (('bx2', 1, 4), ('bx2', -1, 4), ('az4', 1, 0), ('az4', 1, 1), ('az4', 1, 2), ('az4', -1, 0), ('az4', -1, 1), ('az4', -1, 2)), (('sh', 4),)),
    (('mma', 4, 0), (), ()),
    (('mma', 4, 1), (), ()),
    (('mma', 4, 2), (), ()),
    (('mma', 4, 3), (), ()),
    (('mma', 4, 4), (), ()),
    (('settle', 5), (), ()),
    (('mmb', 4, 0), (('sh', 4),), ()),
    (('collect', 2), (('part', 1, 2), ('part', -1, 2), ('part', 2, 2)), ()),
    (('mmb', 4, 1), (), ()),
    (('mmb', 4, 2), (), ()),
    (('mmb', 4, 3), (), ()),
    (('mmb', 4, 4), (), ()),
    (('scatter', 4), (), (('part', 2, 4), ('part', 1, 4), ('part', -1, 4))),
    (('tot', 4), (), (('tot', 1), ('tot', -1), ('tot', 2))),
    (('settle', 7), (), ()),
    (('collect', 3), (('part', 1, 3), ('part', -1, 3), ('part', 2, 3)), ()),
    (('settle', 4), (), ()),
    (('collect', 4), (('part', 1, 4), ('part', -1, 4), ('part', 2, 4)), ()),
)


def split(v):
    hi = v.astype(bf16)
    return hi, (v - hi.astype(f32)).astype(bf16)


def dot3(a, b, dims):
    (ah, al), (bh, bl) = a, b

    def one(u, v):
        return lax.dot_general(u, v, (dims, ((), ())), preferred_element_type=f32)

    out = one(ah, bh) + one(ah, bl)
    return out if al is None else out + one(al, bh)


def precondition(q_ref, bo_ref, bi_ref, eig_ref, bd, mid, out):
    bi = bi_ref[...]
    bd[...] = jnp.zeros((128, 128), f32)
    bd[0:64, 0:64] = bi
    bd[64:128, 64:128] = bi
    even, odd = bo_ref[pl.ds(0, 32, stride=2), :], bo_ref[pl.ds(1, 32, stride=2), :]
    q = q_ref[...]
    rows = jnp.concatenate(
        [q[:, b * BLOCK : (b + 1) * BLOCK].astype(f32) for b in range(BLOCKS)], axis=0
    ).astype(bf16)
    bds = split(bd[...])
    mid[...] = dot3((rows, None), bds, ((1,), (0,)))
    t1 = jnp.concatenate([mid[pl.ds(n, BLOCKS, stride=QDEV), :] for n in range(QDEV)], axis=1)
    y = dot3(split(jnp.concatenate([even, odd], axis=1).T), split(t1), ((1,), (0,)))
    low = lax.broadcasted_iota(jnp.int32, (64, 128), 1) < 64
    eig = jnp.concatenate([eig_ref[...], eig_ref[...]], axis=1)
    parts = []
    for n in range(QDEV):
        lanes = slice(n * 128, (n + 1) * 128)
        s = jnp.where(low, y[0:64, lanes], y[64:128, lanes])
        parts.append((s + pltpu.roll(s, 64, 1)) / eig)
    u = jnp.concatenate(parts, axis=1)
    v = dot3(split(jnp.concatenate([even, odd], axis=0)), split(u), ((1,), (0,)))
    low32 = lax.broadcasted_iota(jnp.int32, (32, 128), 1) < 64
    for n in range(QDEV):
        lanes = slice(n * 128, (n + 1) * 128)
        mid[pl.ds(n, BLOCKS, stride=QDEV), :] = jnp.where(low32, v[0:32, lanes], v[32:64, lanes])
    o = dot3(split(mid[...]), bds, ((1,), (1,)))
    for b in range(BLOCKS):
        out[:, b * BLOCK : (b + 1) * BLOCK] = o[QDEV * b : QDEV * (b + 1)]


def kernel(
    q_hbm, mant_hbm, exps_hbm, bo_hbm, bi_hbm, eig_hbm, asg_hbm,
    scores_hbm, totals_ref,
    q_ref, exps_ref, bo_ref, bi_ref, eig_ref, asg_ref,
    mant, w, p, acc, fac, mask, bd, mid, prep, xch,
    part_out, part_in, sums, tot, tot_in, out,
    ss, rs, ls, ms, os,
):
    e, y = lax.axis_index("ex"), lax.axis_index("lay")
    x, z, c = e // 16, (e // 2) % NZ, e % 2

    def at_x(d):
        return {"ex": (((x + d + NX) % NX) * NZ + z) * 2 + c}

    def at_z(d):
        return {"ex": (x * NZ + (z + d + NZ) % NZ) * 2 + c}

    def at_y(d):
        return {"lay": (y + d + NY) % NY}

    sibling = {"ex": (x * NZ + z) * 2 + 1 - c}

    small = [
        pltpu.make_async_copy(a, b, ls.at[i])
        for i, (a, b) in enumerate(
            (
                (q_hbm, q_ref), (bo_hbm, bo_ref), (bi_hbm, bi_ref),
                (eig_hbm, eig_ref), (exps_hbm, exps_ref), (asg_hbm, asg_ref),
            )
        )
    ]
    for cp in small:
        cp.start()
    loads = [
        pltpu.make_async_copy(
            mant_hbm.at[pl.ds(i * TCH, TCH)], mant.at[pl.ds(i * TCH, TCH)], ms.at[i]
        )
        for i in range(NCH)
    ]
    for cp in loads:
        cp.start()
    barrier = pltpu.get_barrier_semaphore()
    partners = [at_x(d) for d in (1, -1, 2)] + [at_y(d) for d in (1, -1, 2)]
    partners += [at_z(d * k) for k in (1, 2, 3) for d in (1, -1)] + [sibling]
    for dev in partners:
        pl.semaphore_signal(barrier, inc=1, device_id=dev, device_id_type=MESH)

    copies, live = {}, []

    def remote(name, src, dst, dev):
        i = len(copies)
        copies[name] = pltpu.make_async_remote_copy(
            src_ref=src, dst_ref=dst, send_sem=ss.at[i], recv_sem=rs.at[i],
            device_id=dev, device_id_type=MESH,
        )

    def send(*name):
        copies[name].start()
        live.append(name)

    def arrived(*name):
        copies[name].wait_recv()

    def settle(keep=0):
        while len(live) > keep:
            copies[live.pop(0)].wait_send()

    def lanes(first, count):
        return pl.ds(pl.multiple_of(c * HALF + first, 128), count)

    la, lb, lhalf = lanes(0, KA), lanes(KA, KB), lanes(0, HALF)
    for d in (1, -1):
        hi = 0 if d == 1 else 1
        la2 = lanes(hi * (KA // 2), KA // 2)
        lb2 = lanes(KA + hi * (KB // 2), KB // 2)
        hops = [ZSLOT[(-d * k) % NZ] for k in (0, 1, 2, 3)]
        for k in (1, 2, 3):
            via = k - 1 if k in Z_STEP else 0
            remote(
                ("bz", d, k), p.at[hops[via], 0, :, lb], p.at[hops[k], 0, :, lb], at_z(d * (k - via))
            )
        remote(("bz4", d), p.at[hops[3], 0, :, lb2], p.at[ZSLOT[4], 0, :, lb2], at_z(d))
        for i, (first, count) in enumerate(XBLK):
            blk = pl.ds(first, count)
            for k in (1, 2, 3):
                via = k - 1 if k in A_STEP else 0
                remote(
                    ("az", d, i, k),
                    p.at[hops[via], blk, :, la], p.at[hops[k], blk, :, la], at_z(d * (k - via)),
                )
            remote(("az4", d, i), p.at[hops[3], blk, :, la2], p.at[ZSLOT[4], blk, :, la2], at_z(d))
        near = XSLOT[(-d) % NX]
        for i, (first, count) in enumerate(DIST):
            blk = pl.ds(first, count)
            remote(("bx", d, i), p.at[blk, 0, :, lb], p.at[blk, near, :, lb], at_x(d))
            if i not in X_FAR:
                remote(("bx2", d, i), p.at[blk, near, :, lb2], p.at[blk, 3, :, lb2], at_x(d))
            elif d == 1:
                remote(("bx2", 2, i), p.at[blk, 0, :, lb], p.at[blk, 3, :, lb], at_x(2))
        remote(("ax", d), p.at[0, 0, :, la], p.at[0, near, :, la], at_x(d))
    remote(("ax", 2), p.at[0, 0, :, la], p.at[0, 3, :, la], at_x(2))
    for g, (first, count) in enumerate(GROUP):
        blk = pl.ds(first, count)
        remote(("sh", g), p.at[blk, :, :, lhalf], p.at[blk, :, :, lhalf], sibling)
        for i, d in enumerate((1, -1, 2)):
            remote(("part", d, g), part_out.at[i, blk], part_in.at[i, blk], at_y(d))
    for i, d in enumerate((1, -1, 2)):
        remote(("tot", d), tot, tot_in.at[i], at_y(d))
    other_cols = pl.ds(pl.multiple_of((1 - c) * HALF, HALF), HALF)
    own_cols = pl.ds(pl.multiple_of(c * HALF, HALF), HALF)
    remote(("swap",), prep.at[:, other_cols], xch.at[c], sibling)

    for cp in small:
        cp.wait()
    precondition(q_ref, bo_ref, bi_ref, eig_ref, bd, mid, prep)
    pl.semaphore_wait(barrier, len(partners))
    send("swap")
    exps = exps_ref[...]
    factor = jnp.zeros(exps.shape, f32)
    for exponent in range(lowest_exponent, highest_exponent):
        factor = factor + jnp.where(exps == exponent, f32(2.0**exponent), f32(0.0))
    fac[...] = factor
    for i in range(NX):
        one = (asg_ref[:, i * 128 : (i + 1) * 128] == 1).astype(f32)
        mask[i] = jnp.broadcast_to(one, (128, 128)).T

    def dequantize(i):
        loads[i].wait()
        t = pl.ds(i * TCH, TCH)
        for b in range(BLOCKS):
            rows = pl.ds(b * BLOCK, BLOCK)
            w[rows, t] = mant[t, rows].T * fac[b : b + 1, t].astype(bf16)

    def multiply(g, n, part):
        first, count = GROUP[g]
        blk = pl.ds(first, count)
        k = pl.ds(pl.multiple_of((c if part == 0 else 1 - c) * HALF, HALF), HALF)
        cols = pl.ds(n * NT, NT)
        rows = count * NX * PAIR
        a = p[blk, :, :, k].reshape(rows, HALF)
        if rows < 128:
            a = jnp.concatenate([a, jnp.zeros((128 - rows, HALF), bf16)], axis=0)
        r = jnp.dot(a, w[k, cols], preferred_element_type=f32)[0:rows]
        r = r.reshape(count, NX, PAIR, NT)
        acc[blk, :, :, cols] = r if part == 0 else acc[blk, :, :, cols] + r

    def slot_of(d):
        xr = (y + d + NY - x + NX) % NX
        return xr + xr // 2 - 2 * (xr // 3)

    def add_totals(g):
        t0, t1 = None, None
        first, count = GROUP[g]
        for s in range(first, first + count):
            zo = (z + ZORDER[s]) % NZ
            for j in range(NX):
                xo = (x + XORDER[j]) % NX
                m = mask[xo, pl.ds(pl.multiple_of(zo * PAIR, PAIR), PAIR), :]
                m = jnp.concatenate([m] * (ROWS // 128), axis=1)
                v = acc[s, j]
                p1 = v * m
                p0 = v - p1
                p0, p1 = p0[0:8] + p0[8:16], p1[0:8] + p1[8:16]
                t0, t1 = (p0, p1) if t0 is None else (t0 + p0, t1 + p1)
        for i, t in enumerate((t0, t1)):
            sums[i] = t if g == 0 else sums[i] + t
        if g == len(GROUP) - 1:
            tot[...] = jnp.zeros(tot.shape, f32)
            for i in range(2):
                total = jnp.sum(sums[i], axis=0, keepdims=True)
                for n in range(ROWS // NT):
                    tot[8 * i + n : 8 * i + n + 1, :] = total[:, n * NT : (n + 1) * NT]

    def scatter(g):
        first, count = GROUP[g]
        for i, d in ((2, 2), (0, 1), (1, -1)):
            to = slot_of(d)
            for s in range(first, first + count):
                part_out[i, s] = acc[s, to].astype(bf16)

    normalizer = 1.0 / math.sqrt(NY * ENTRIES)
    stores = []

    def collect(g):
        mine = slot_of(0)
        first, count = GROUP[g]
        for s in range(first, first + count):
            total = acc[s, mine] + part_in[0, s].astype(f32)
            total = total + part_in[1, s].astype(f32) + part_in[2, s].astype(f32)
            out[s] = total * normalizer
            zo = (z + ZORDER[s]) % NZ
            cp = pltpu.make_async_copy(
                out.at[s],
                scores_hbm.at[pl.ds(pl.multiple_of(zo * PAIR, PAIR), PAIR)],
                os.at[s],
            )
            cp.start()
            stores.append(cp)

    do = {
        "copy": lambda: None, "settle": lambda n: settle(max(len(live) - n, 0)),
        "dq": lambda i: None if i < EARLY else dequantize(i),
        "mma": lambda g, n: multiply(g, n, 0), "mmb": lambda g, n: multiply(g, n, 1),
        "scatter": scatter, "tot": add_totals, "collect": collect,
    }
    xch[c] = prep[:, own_cols]
    for i in range(EARLY):
        dequantize(i)
    arrived("swap")
    p[0, 0, :, lhalf] = xch[...].reshape(PAIR, HALF).astype(bf16)
    for (step, *args), waits, sends in STEPS:
        for name in waits:
            arrived(*name)
        do[step](*args)
        for name in sends:
            send(*name)
    for d in (1, -1, 2):
        arrived("tot", d)
    total = tot[...] + tot_in[0] + tot_in[1] + tot_in[2]
    for i in range(2):
        for n in range(ROWS // NT):
            row = total[8 * i + n : 8 * i + n + 1, :]
            totals_ref[i : i + 1, n * NT : (n + 1) * NT] = row * (normalizer / math.sqrt(QB))
    settle()
    for cp in stores:
        cp.wait()


N_COPIES = 2 * (3 + 1 + 4 * len(XBLK) + 10 + 1) - len(X_FAR) + 1 + 4 * len(GROUP) + 3 + 1


def body(queries, train_mantissa, scale_exponents, basis_out, basis_in, eigen, assignment):
    hbm = pl.BlockSpec(memory_space=pl.ANY)
    vmem = pltpu.VMEM
    dma = pltpu.SemaphoreType.DMA
    piece = (3, NZ, PAIR, ROWS)
    scores, totals = pl.pallas_call(
        kernel,
        out_shape=(
            jax.ShapeDtypeStruct((NX * 32, ROWS), f32),
            jax.ShapeDtypeStruct((2, ROWS), f32),
        ),
        in_specs=[hbm] * 7,
        out_specs=(hbm, pl.BlockSpec(memory_space=pltpu.VMEM)),
        scratch_shapes=[
            vmem((QDEV, ENTRIES), bf16),
            vmem((BLOCKS, ROWS), jnp.int32),
            vmem((ORDER, ORDER), f32),
            vmem((ORDER, ORDER), f32),
            vmem((ORDER, ORDER), f32),
            vmem((1, 512), jnp.int32),
            vmem((ROWS, ENTRIES), bf16),
            vmem((ENTRIES, ROWS), bf16),
            vmem((NZ, NX, PAIR, ENTRIES), bf16),
            vmem((NZ, NX, PAIR, ROWS), f32),
            vmem((BLOCKS, ROWS), f32),
            vmem((NX, 128, 128), f32),
            vmem((128, 128), f32),
            vmem((BLOCKS * QDEV, 128), f32),
            vmem((QDEV, ENTRIES), f32),
            vmem((2, QDEV, HALF), f32),
            vmem(piece, bf16),
            vmem(piece, bf16),
            vmem((2, 8, ROWS), f32),
            vmem((16, NT), f32),
            vmem((3, 16, NT), f32),
            vmem((NZ, PAIR, ROWS), f32),
            dma((N_COPIES,)),
            dma((N_COPIES,)),
            dma((6,)),
            dma((NCH,)),
            dma((NZ,)),
        ],
        compiler_params=pltpu.CompilerParams(
            collective_id=0, has_side_effects=True, vmem_limit_bytes=56 * 2**20
        ),
        name="influence",
    )(
        queries.reshape(QDEV, ENTRIES),
        train_mantissa.reshape(ROWS, ENTRIES),
        scale_exponents.reshape(ROWS, BLOCKS).T,
        basis_out.reshape(ORDER, ORDER),
        basis_in.reshape(ORDER, ORDER),
        eigen.reshape(ORDER, ORDER),
        assignment.reshape(1, 512),
    )
    return scores, totals


def solution(mesh):
    placed = (
        P("ex", "lay", None),
        P("ex", "lay", None),
        P("ex", "lay", None),
        P("lay", None, None),
        P("lay", None, None),
        P("lay", None, None),
        P(),
    )
    return jax.shard_map(
        body, mesh=mesh, in_specs=placed, out_specs=(P("lay", "ex"), P(None, "ex")), check_vma=False
    )
```

```python
import math

import jax
import jax.numpy as jnp
from jax import lax
from jax.experimental import pallas as pl
from jax.experimental.pallas import tpu as pltpu
from jax.sharding import PartitionSpec as P

MESH = pl.DeviceIdType.MESH
f32, bf16 = jnp.float32, jnp.bfloat16

NX, NY, NZ = 4, 4, 8
ORDER = 64
ENTRIES = ORDER * ORDER
HALF = ENTRIES // 2
BLOCKS = 32
BLOCK = ENTRIES // BLOCKS
ROWS = 1280
QDEV = 8
PAIR = 16
KA = 1024
KB = HALF - KA
NT = 256
HT = ROWS // 2
TCH = 128
NCH = ROWS // TCH
EARLY = 2
QB = 256
lowest_exponent = -2
highest_exponent = 2

ZORDER = (0, 1, 7, 2, 6, 3, 5, 4)
ZSLOT = {zr: i for i, zr in enumerate(ZORDER)}
XORDER = (0, 1, 3, 2)
XSLOT = {xr: i for i, xr in enumerate(XORDER)}
XBLK = ((0, 1), (1, 2), (3, 1))
DIST = ((0, 1), (1, 2), (3, 2), (5, 2), (7, 1))
GROUP = ((0, 1), (1, 2), (3, 2), (5, 2), (7, 1))
Z_STEP = (2, 3)
A_STEP = (2, 3)
X_FAR = (0, 1, 2, 3, 4)
Z_FAR, A_FAR = (0, 0)
VIA = ()
STEPS = (
    (('copy',), (), (('bz', 1, 1), ('bz', -1, 1), ('bx', 1, 0), ('bx', -1, 0), ('bx2', 2, 0), ('ax', 1), ('ax', -1), ('ax', 2), ('az', 1, 0, 1), ('az', -1, 0, 1))),
    (('dq', 0), (), ()),
    (('dq', 1), (), ()),
    (('dq', 2), (), ()),
    (('dq', 3), (), ()),
    (('dq', 4), (), ()),
    (('dq', 5), (), ()),
    (('dq', 6), (), ()),
    (('dq', 7), (), ()),
    (('copy',), (('bz', 1, 1),), (('bz', 1, 2),)),
    (('copy',), (('bz', -1, 1),), (('bx', 1, 1), ('bx', -1, 1), ('bx2', 2, 1))),
    (('copy',), (), (('bz', -1, 2),)),
    (('dq', 8), (), ()),
    (('copy',), (('az', 1, 0, 1),), (('az', 1, 0, 2),)),
    (('copy',), (('az', -1, 0, 1),), (('az', -1, 0, 2),)),
    (('dq', 9), (), ()),
    (('copy',), (('ax', 1), ('ax', -1)), (('az', 1, 1, 1), ('az', -1, 1, 1))),
    (('copy',), (('bx', 1, 0), ('bx', -1, 0), ('bx2', 2, 0)), (('shb', 0),)),
    (('copy',), (('ax', 2),), (('sha', 0),)),
    (('copy',), (), (('az', 1, 2, 1), ('az', -1, 2, 1))),
    (('mma', 0, 0), (), ()),
    (('mma', 0, 1), (), ()),
    (('mma', 0, 2), (), ()),
    (('copy',), (('bz', 1, 2),), (('bz', 1, 3),)),
    (('mma', 0, 3), (), ()),
    (('copy',), (('bz', -1, 2),), (('bx', 1, 2), ('bx', -1, 2), ('bx2', 2, 2))),
    (('copy',), (), (('bz', -1, 3),)),
    (('mma', 0, 4), (), ()),
    (('copy',), (('az', 1, 0, 2),), (('az', 1, 0, 3),)),
    (('copy',), (('az', -1, 0, 2),), (('az', -1, 0, 3),)),
    (('settle', 5), (), ()),
    (('mmb', 0, 0), (('sha', 0), ('shb', 0)), ()),
    (('mmb', 0, 1), (), ()),
    (('mmb', 0, 2), (), ()),
    (('mmb', 0, 3), (), ()),
    (('mmb', 0, 4), (), ()),
    (('scatter', 0), (), (('part', 2, 0), ('part', 1, 0), ('part', -1, 0))),
    (('copy',), (('bx', 1, 1), ('bx', -1, 1), ('bx2', 2, 1)), (('shb', 1),)),
    (('copy',), (('az', -1, 1, 1),), (('az', -1, 1, 2),)),
    (('copy',), (('az', 1, 1, 1),), (('az', 1, 1, 2),)),
    (('tot', 0), (), ()),
    (('settle', 5), (), ()),
    (('copy',), (('az', 1, 2, 1),), (('az', 1, 2, 2),)),
    (('copy',), (('az', -1, 2, 1),), (('sha', 1),)),
    (('copy',), (), (('az', -1, 2, 2),)),
    (('mma', 1, 0), (), ()),
    (('mma', 1, 1), (), ()),
    (('mma', 1, 2), (), ()),
    (('copy',), (('bz', 1, 3),), (('bz4', 1),)),
    (('mma', 1, 3), (), ()),
    (('copy',), (('bz', -1, 3),), (('bz4', -1),)),
    (('copy',), (), (('bx', 1, 3), ('bx', -1, 3), ('bx2', 2, 3))),
    (('mma', 1, 4), (), ()),
    (('copy',), (('az', 1, 0, 3),), (('az4', 1, 0),)),
    (('copy',), (('az', -1, 0, 3),), (('az4', -1, 0),)),
    (('settle', 10), (), ()),
    (('copy',), (('bx', 1, 2), ('bx', -1, 2), ('bx2', 2, 2)), (('shb', 2),)),
    (('mmb', 1, 0), (('sha', 1), ('shb', 1)), ()),
    (('mmb', 1, 1), (), ()),
    (('mmb', 1, 2), (), ()),
    (('copy',), (('az', 1, 1, 2),), (('az', 1, 1, 3),)),
    (('copy',), (('az', -1, 1, 2),), (('az', -1, 1, 3),)),
    (('mmb', 1, 3), (), ()),
    (('mmb', 1, 4), (), ()),
    (('scatter', 1), (), (('part', 2, 1), ('part', 1, 1), ('part', -1, 1))),
    (('copy',), (('az', 1, 2, 2),), (('az', 1, 2, 3),)),
    (('copy',), (('az', -1, 2, 2),), (('az', -1, 2, 3),)),
    (('copy',), (), (('sha', 2),)),
    (('mma', 2, 0), (), ()),
    (('mma', 2, 1), (), ()),
    (('copy',), (('bz4', 1), ('bz4', -1)), (('bx', 1, 4), ('bx', -1, 4), ('bx2', 2, 4))),
    (('tot', 1), (), ()),
    (('mma', 2, 2), (), ()),
    (('mma', 2, 3), (), ()),
    (('mma', 2, 4), (), ()),
    (('collect', 0), (('part', 1, 0), ('part', -1, 0), ('part', 2, 0)), ()),
    (('settle', 16), (), ()),
    (('copy',), (('bx', 1, 3), ('bx', -1, 3), ('bx2', 2, 3)), (('shb', 3),)),
    (('mmb', 2, 0), (('sha', 2), ('shb', 2)), ()),
    (('mmb', 2, 1), (), ()),
    (('copy',), (('az', 1, 1, 3),), (('az4', 1, 1),)),
    (('mmb', 2, 2), (), ()),
    (('copy',), (('az', -1, 1, 3),), (('az4', -1, 1),)),
    (('mmb', 2, 3), (), ()),
    (('mmb', 2, 4), (), ()),
    (('scatter', 2), (), (('part', 2, 2), ('part', 1, 2), ('part', -1, 2))),
    (('copy',), (('az', -1, 2, 3),), (('az4', -1, 2),)),
    (('copy',), (('az', 1, 2, 3),), (('sha', 3),)),
    (('mma', 3, 0), (), ()),
    (('copy',), (), (('az4', 1, 2),)),
    (('mma', 3, 1), (), ()),
    (('mma', 3, 2), (), ()),
    (('copy',), (('bx', 1, 4), ('bx', -1, 4), ('bx2', 2, 4)), (('shb', 4),)),
    (('tot', 2), (), ()),
    (('mma', 3, 3), (), ()),
    (('mma', 3, 4), (), ()),
    (('settle', 8), (), ()),
    (('collect', 1), (('part', 1, 1), ('part', -1, 1), ('part', 2, 1)), ()),
    (('settle', 5), (), ()),
    (('mmb', 3, 0), (('sha', 3), ('shb', 3)), ()),
    (('mmb', 3, 1), (), ()),
    (('copy',), (('az4', 1, 0), ('az4', -1, 0), ('az4', 1, 1), ('az4', -1, 1), ('az4', 1, 2), ('az4', -1, 2)), (('sha', 4),)),
    (('mmb', 3, 2), (), ()),
    (('mmb', 3, 3), (), ()),
    (('mmb', 3, 4), (), ()),
    (('scatter', 3), (), (('part', 2, 3), ('part', 1, 3), ('part', -1, 3))),
    (('mma', 4, 0), (), ()),
    (('mma', 4, 1), (), ()),
    (('mma', 4, 2), (), ()),
    (('mma', 4, 3), (), ()),
    (('mma', 4, 4), (), ()),
    (('tot', 3), (), ()),
    (('mmb', 4, 0), (('sha', 4), ('shb', 4)), ()),
    (('mmb', 4, 1), (), ()),
    (('mmb', 4, 2), (), ()),
    (('mmb', 4, 3), (), ()),
    (('mmb', 4, 4), (), ()),
    (('scatter', 4), (), (('part', 2, 4), ('part', 1, 4), ('part', -1, 4))),
    (('collect', 2), (('part', 1, 2), ('part', -1, 2), ('part', 2, 2)), ()),
    (('tot', 4), (), (('tot', 1), ('tot', -1), ('tot', 2))),
    (('settle', 20), (), ()),
    (('collect', 3), (('part', 1, 3), ('part', -1, 3), ('part', 2, 3)), ()),
    (('settle', 3), (), ()),
    (('collect', 4), (('part', 1, 4), ('part', -1, 4), ('part', 2, 4)), ()),
)


def split(v):
    hi = v.astype(bf16)
    return hi, (v - hi.astype(f32)).astype(bf16)


def dot3(a, b, dims):
    (ah, al), (bh, bl) = a, b

    def one(u, v):
        return lax.dot_general(u, v, (dims, ((), ())), preferred_element_type=f32)

    out = one(ah, bh) + one(ah, bl)
    return out if al is None else out + one(al, bh)


def precondition(q_ref, bo_ref, bi_ref, eig_ref, bd, mid, out):
    bi = bi_ref[...]
    bd[...] = jnp.zeros((128, 128), f32)
    bd[0:64, 0:64] = bi
    bd[64:128, 64:128] = bi
    even, odd = bo_ref[pl.ds(0, 32, stride=2), :], bo_ref[pl.ds(1, 32, stride=2), :]
    q = q_ref[...]
    rows = jnp.concatenate(
        [q[:, b * BLOCK : (b + 1) * BLOCK].astype(f32) for b in range(BLOCKS)], axis=0
    ).astype(bf16)
    bds = split(bd[...])
    mid[...] = dot3((rows, None), bds, ((1,), (0,)))
    t1 = jnp.concatenate([mid[pl.ds(n, BLOCKS, stride=QDEV), :] for n in range(QDEV)], axis=1)
    y = dot3(split(jnp.concatenate([even, odd], axis=1).T), split(t1), ((1,), (0,)))
    low = lax.broadcasted_iota(jnp.int32, (64, 128), 1) < 64
    eig = jnp.concatenate([eig_ref[...], eig_ref[...]], axis=1)
    parts = []
    for n in range(QDEV):
        lanes = slice(n * 128, (n + 1) * 128)
        s = jnp.where(low, y[0:64, lanes], y[64:128, lanes])
        parts.append((s + pltpu.roll(s, 64, 1)) / eig)
    u = jnp.concatenate(parts, axis=1)
    v = dot3(split(jnp.concatenate([even, odd], axis=0)), split(u), ((1,), (0,)))
    low32 = lax.broadcasted_iota(jnp.int32, (32, 128), 1) < 64
    for n in range(QDEV):
        lanes = slice(n * 128, (n + 1) * 128)
        mid[pl.ds(n, BLOCKS, stride=QDEV), :] = jnp.where(low32, v[0:32, lanes], v[32:64, lanes])
    o = dot3(split(mid[...]), bds, ((1,), (1,)))
    for b in range(BLOCKS):
        out[:, b * BLOCK : (b + 1) * BLOCK] = o[QDEV * b : QDEV * (b + 1)]


def kernel(
    q_hbm, mant_hbm, exps_hbm, bo_hbm, bi_hbm, eig_hbm, asg_hbm,
    scores_ref, totals_ref,
    q_ref, exps_ref, bo_ref, bi_ref, eig_ref, asg_ref,
    mant, w, p, acc, fac, mask, bd, mid, prep, xch,
    part_out, part_in, sums, tot, tot_in,
    ss, rs, ls, ms,
):
    e, y = lax.axis_index("ex"), lax.axis_index("lay")
    x, z, c = e // 16, (e // 2) % NZ, e % 2

    def at_x(d):
        return {"ex": (((x + d + NX) % NX) * NZ + z) * 2 + c}

    def at_z(d):
        return {"ex": (x * NZ + (z + d + NZ) % NZ) * 2 + c}

    def at_y(d):
        return {"lay": (y + d + NY) % NY}

    sibling = {"ex": (x * NZ + z) * 2 + 1 - c}

    small = [
        pltpu.make_async_copy(a, b, ls.at[i])
        for i, (a, b) in enumerate(
            (
                (q_hbm, q_ref), (bo_hbm, bo_ref), (bi_hbm, bi_ref),
                (eig_hbm, eig_ref), (exps_hbm, exps_ref), (asg_hbm, asg_ref),
            )
        )
    ]
    for cp in small:
        cp.start()
    loads = [
        pltpu.make_async_copy(
            mant_hbm.at[pl.ds(i * TCH, TCH)], mant.at[pl.ds(i * TCH, TCH)], ms.at[i]
        )
        for i in range(NCH)
    ]
    for cp in loads:
        cp.start()
    barrier = pltpu.get_barrier_semaphore()
    partners = [at_x(d) for d in (1, -1, 2)] + [at_y(d) for d in (1, -1, 2)]
    steps = {1} | {k for k in (2, 3) if k not in Z_STEP or k not in A_STEP}
    partners += [at_z(d * k) for k in sorted(steps) for d in (1, -1)] + [sibling]
    if Z_FAR or A_FAR:
        partners.append(at_z(4))
    for dev in partners:
        pl.semaphore_signal(barrier, inc=1, device_id=dev, device_id_type=MESH)

    copies, live = {}, []

    def remote(name, src, dst, dev):
        i = len(copies)
        copies[name] = pltpu.make_async_remote_copy(
            src_ref=src, dst_ref=dst, send_sem=ss.at[i], recv_sem=rs.at[i],
            device_id=dev, device_id_type=MESH,
        )

    def send(*name):
        copies[name].start()
        live.append(name)

    def arrived(*name):
        copies[name].wait_recv()

    def settle(keep=0):
        while len(live) > keep:
            copies[live.pop(0)].wait_send()

    def lanes(first, count):
        return pl.ds(pl.multiple_of(c * HALF + first, 128), count)

    la, lb, lhalf = lanes(0, KA), lanes(KA, KB), lanes(0, HALF)
    for d in (1, -1):
        hi = 0 if d == 1 else 1
        la2 = lanes(hi * (KA // 2), KA // 2)
        lb2 = lanes(KA + hi * (KB // 2), KB // 2)
        hops = [ZSLOT[(-d * k) % NZ] for k in (0, 1, 2, 3)]
        for k in (1, 2, 3):
            via = k - 1 if k in Z_STEP else 0
            remote(
                ("bz", d, k), p.at[hops[via], 0, :, lb], p.at[hops[k], 0, :, lb], at_z(d * (k - via))
            )
        if not Z_FAR:
            remote(("bz4", d), p.at[hops[3], 0, :, lb2], p.at[ZSLOT[4], 0, :, lb2], at_z(d))
        elif d == 1:
            remote(("bz4", 2), p.at[0, 0, :, lb], p.at[ZSLOT[4], 0, :, lb], at_z(4))
        for i, (first, count) in enumerate(XBLK):
            blk = pl.ds(first, count)
            for k in (1, 2, 3):
                via = k - 1 if k in A_STEP else 0
                remote(
                    ("az", d, i, k),
                    p.at[hops[via], blk, :, la], p.at[hops[k], blk, :, la], at_z(d * (k - via)),
                )
            if not A_FAR:
                remote(
                    ("az4", d, i), p.at[hops[3], blk, :, la2], p.at[ZSLOT[4], blk, :, la2], at_z(d)
                )
            elif d == 1:
                remote(("az4", 2, i), p.at[0, blk, :, la], p.at[ZSLOT[4], blk, :, la], at_z(4))
        near = XSLOT[(-d) % NX]
        for i, (first, count) in enumerate(DIST):
            blk = pl.ds(first, count)
            remote(("bx", d, i), p.at[blk, 0, :, lb], p.at[blk, near, :, lb], at_x(d))
            if i not in X_FAR:
                remote(("bx2", d, i), p.at[blk, near, :, lb2], p.at[blk, 3, :, lb2], at_x(d))
            elif d == 1:
                remote(("bx2", 2, i), p.at[blk, 0, :, lb], p.at[blk, 3, :, lb], at_x(2))
        remote(("ax", d), p.at[0, 0, :, la], p.at[0, near, :, la], at_x(d))
    remote(("ax", 2), p.at[0, 0, :, la], p.at[0, 3, :, la], at_x(2))
    for g, (first, count) in enumerate(GROUP):
        blk = pl.ds(first, count)
        remote(("sha", g), p.at[blk, :, :, la], p.at[blk, :, :, la], sibling)
        remote(("shb", g), p.at[blk, :, :, lb], p.at[blk, :, :, lb], sibling)
        if g in VIA:
            for i, d in enumerate((1, -1)):
                t = pl.ds(i * HT, HT)
                remote(
                    ("y2", d, g), part_out.at[2, blk, :, t], part_in.at[2, blk, :, t], at_y(d)
                )
                remote(("y1", d, g), part_out.at[i, blk], part_in.at[i, blk], at_y(d))
        else:
            for i, d in enumerate((1, -1, 2)):
                remote(("part", d, g), part_out.at[i, blk], part_in.at[i, blk], at_y(d))
    for i, d in enumerate((1, -1, 2)):
        remote(("tot", d), tot, tot_in.at[i], at_y(d))
    other_cols = pl.ds(pl.multiple_of((1 - c) * HALF, HALF), HALF)
    own_cols = pl.ds(pl.multiple_of(c * HALF, HALF), HALF)
    remote(("swap",), prep.at[:, other_cols], xch.at[c], sibling)

    for cp in small:
        cp.wait()
    precondition(q_ref, bo_ref, bi_ref, eig_ref, bd, mid, prep)
    pl.semaphore_wait(barrier, len(partners))
    send("swap")
    exps = exps_ref[...]
    factor = jnp.zeros(exps.shape, f32)
    for exponent in range(lowest_exponent, highest_exponent):
        factor = factor + jnp.where(exps == exponent, f32(2.0**exponent), f32(0.0))
    fac[...] = factor
    for i in range(NX):
        one = (asg_ref[:, i * 128 : (i + 1) * 128] == 1).astype(f32)
        mask[i] = jnp.broadcast_to(one, (128, 128)).T

    def dequantize(i):
        loads[i].wait()
        t = pl.ds(i * TCH, TCH)
        for b in range(BLOCKS):
            rows = pl.ds(b * BLOCK, BLOCK)
            w[rows, t] = mant[t, rows].T * fac[b : b + 1, t].astype(bf16)

    def multiply(g, n, part):
        first, count = GROUP[g]
        blk = pl.ds(first, count)
        k = pl.ds(pl.multiple_of((c if part == 0 else 1 - c) * HALF, HALF), HALF)
        cols = pl.ds(n * NT, NT)
        rows = count * NX * PAIR
        a = p[blk, :, :, k].reshape(rows, HALF)
        if rows < 128:
            a = jnp.concatenate([a, jnp.zeros((128 - rows, HALF), bf16)], axis=0)
        r = jnp.dot(a, w[k, cols], preferred_element_type=f32)[0:rows]
        r = r.reshape(count, NX, PAIR, NT)
        acc[blk, :, :, cols] = r if part == 0 else acc[blk, :, :, cols] + r

    def slot_of(d):
        xr = (y + d + NY - x + NX) % NX
        return xr + xr // 2 - 2 * (xr // 3)

    def add_totals(g):
        t0, t1 = None, None
        first, count = GROUP[g]
        for s in range(first, first + count):
            zo = (z + ZORDER[s]) % NZ
            for j in range(NX):
                xo = (x + XORDER[j]) % NX
                m = mask[xo, pl.ds(pl.multiple_of(zo * PAIR, PAIR), PAIR), :]
                m = jnp.concatenate([m] * (ROWS // 128), axis=1)
                v = acc[s, j]
                p1 = v * m
                p0 = v - p1
                p0, p1 = p0[0:8] + p0[8:16], p1[0:8] + p1[8:16]
                t0, t1 = (p0, p1) if t0 is None else (t0 + p0, t1 + p1)
        for i, t in enumerate((t0, t1)):
            sums[i] = t if g == 0 else sums[i] + t
        if g == len(GROUP) - 1:
            tot[...] = jnp.zeros(tot.shape, f32)
            for i in range(2):
                total = jnp.sum(sums[i], axis=0, keepdims=True)
                for n in range(ROWS // NT):
                    tot[8 * i + n : 8 * i + n + 1, :] = total[:, n * NT : (n + 1) * NT]

    def scatter(g):
        first, count = GROUP[g]
        for i, d in ((2, 2),) if g in VIA else ((2, 2), (0, 1), (1, -1)):
            to = slot_of(d)
            for s in range(first, first + count):
                part_out[i, s] = acc[s, to].astype(bf16)

    def combine(g):
        first, count = GROUP[g]
        for i, d in ((0, 1), (1, -1)):
            to = slot_of(d)
            for j in range(2):
                t = pl.ds(j * HT, HT)
                for s in range(first, first + count):
                    v = acc[s, to, :, t]
                    v = v + part_in[2, s, :, t].astype(f32) if i == j else v
                    part_out[i, s, :, t] = v.astype(bf16)

    normalizer = 1.0 / math.sqrt(NY * ENTRIES)

    def collect(g):
        mine = slot_of(0)
        first, count = GROUP[g]
        for s in range(first, first + count):
            total = acc[s, mine] + part_in[0, s].astype(f32)
            total = total + part_in[1, s].astype(f32)
            if g not in VIA:
                total = total + part_in[2, s].astype(f32)
            zo = (z + ZORDER[s]) % NZ
            scores_ref[pl.ds(pl.multiple_of(zo * PAIR, PAIR), PAIR), :] = total * normalizer

    do = {
        "copy": lambda: None, "settle": lambda n: settle(max(len(live) - n, 0)),
        "dq": lambda i: None if i < EARLY else dequantize(i),
        "mma": lambda g, n: multiply(g, n, 0), "mmb": lambda g, n: multiply(g, n, 1),
        "scatter": scatter, "comb": combine, "tot": add_totals, "collect": collect,
    }
    xch[c] = prep[:, own_cols]
    for i in range(EARLY):
        dequantize(i)
    arrived("swap")
    p[0, 0, :, lhalf] = xch[...].reshape(PAIR, HALF).astype(bf16)
    for (step, *args), waits, sends in STEPS:
        for name in waits:
            arrived(*name)
        do[step](*args)
        for name in sends:
            send(*name)
    for d in (1, -1, 2):
        arrived("tot", d)
    total = tot[...] + tot_in[0] + tot_in[1] + tot_in[2]
    for i in range(2):
        for n in range(ROWS // NT):
            row = total[8 * i + n : 8 * i + n + 1, :]
            totals_ref[i : i + 1, n * NT : (n + 1) * NT] = row * (normalizer / math.sqrt(QB))
    settle()


N_COPIES = 2 * (3 + 1 + 4 * len(XBLK) + 10 + 1) - len(X_FAR) - Z_FAR - A_FAR * len(XBLK) + 1 + 5 * len(GROUP) + len(VIA) + 3 + 1


def body(queries, train_mantissa, scale_exponents, basis_out, basis_in, eigen, assignment):
    hbm = pl.BlockSpec(memory_space=pl.ANY)
    vmem = pltpu.VMEM
    dma = pltpu.SemaphoreType.DMA
    piece = (3, NZ, PAIR, ROWS)
    scores, totals = pl.pallas_call(
        kernel,
        out_shape=(
            pltpu.VMEM((NX * 32, ROWS), f32),
            pltpu.VMEM((2, ROWS), f32),
        ),
        in_specs=[hbm] * 7,
        out_specs=(pl.BlockSpec(memory_space=pltpu.VMEM),) * 2,
        scratch_shapes=[
            vmem((QDEV, ENTRIES), bf16),
            vmem((BLOCKS, ROWS), jnp.int32),
            vmem((ORDER, ORDER), f32),
            vmem((ORDER, ORDER), f32),
            vmem((ORDER, ORDER), f32),
            vmem((1, 512), jnp.int32),
            vmem((ROWS, ENTRIES), bf16),
            vmem((ENTRIES, ROWS), bf16),
            vmem((NZ, NX, PAIR, ENTRIES), bf16),
            vmem((NZ, NX, PAIR, ROWS), f32),
            vmem((BLOCKS, ROWS), f32),
            vmem((NX, 128, 128), f32),
            vmem((128, 128), f32),
            vmem((BLOCKS * QDEV, 128), f32),
            vmem((QDEV, ENTRIES), f32),
            vmem((2, QDEV, HALF), f32),
            vmem(piece, bf16),
            vmem(piece, bf16),
            vmem((2, 8, ROWS), f32),
            vmem((16, NT), f32),
            vmem((3, 16, NT), f32),
            dma((N_COPIES,)),
            dma((N_COPIES,)),
            dma((6,)),
            dma((NCH,)),
        ],
        compiler_params=pltpu.CompilerParams(
            collective_id=0, has_side_effects=True, vmem_limit_bytes=56 * 2**20
        ),
        name="influence",
    )(
        queries.reshape(QDEV, ENTRIES),
        train_mantissa.reshape(ROWS, ENTRIES),
        scale_exponents.reshape(ROWS, BLOCKS).T,
        basis_out.reshape(ORDER, ORDER),
        basis_in.reshape(ORDER, ORDER),
        eigen.reshape(ORDER, ORDER),
        assignment.reshape(1, 512),
    )
    return scores, totals


def solution(mesh):
    placed = (
        P("ex", "lay", None),
        P("ex", "lay", None),
        P("ex", "lay", None),
        P("lay", None, None),
        P("lay", None, None),
        P("lay", None, None),
        P(),
    )
    return jax.shard_map(
        body, mesh=mesh, in_specs=placed, out_specs=(P("lay", "ex"), P(None, "ex")), check_vma=False
    )
```

```python
import math

import jax
import jax.numpy as jnp
from jax import lax
from jax.experimental import pallas as pl
from jax.experimental.pallas import tpu as pltpu
from jax.sharding import PartitionSpec as P

MESH = pl.DeviceIdType.MESH
f32, bf16 = jnp.float32, jnp.bfloat16

NX, NY, NZ = 4, 4, 8
ORDER = 64
ENTRIES = ORDER * ORDER
HALF = ENTRIES // 2
BLOCKS = 32
BLOCK = ENTRIES // BLOCKS
ROWS = 1280
QDEV = 8
PAIR = 16
KA = 1024
KB = HALF - KA
NT = 256
HT = ROWS // 2
TCH = 128
NCH = ROWS // TCH
EARLY = 2
(
    COPY, SETTLE, DQ, MMA, MMB, SCATTER, COMB, TOT, COLLECT,
    BZ, BZ4, BX, BX2, AX, AZ, AZ4, SHA, SHB, PART, Y1, Y2, SWAP,
) = range(22)
QB = 256
lowest_exponent = -2
highest_exponent = 2

ZORDER = (0, 1, 7, 2, 6, 3, 5, 4)
ZSLOT = {zr: i for i, zr in enumerate(ZORDER)}
XORDER = (0, 1, 3, 2)
XSLOT = {xr: i for i, xr in enumerate(XORDER)}
XBLK = ((0, 1), (1, 2), (3, 1))
DIST = ((0, 1), (1, 2), (3, 2), (5, 2), (7, 1))
GROUP = ((0, 1), (1, 2), (3, 2), (5, 2), (7, 1))
Z_STEP = (2, 3)
A_STEP = (2, 3)
X_FAR = (0, 1, 2, 3, 4)
Z_FAR, A_FAR = (0, 0)
VIA = ()
STEPS = (
    ((COPY,), (), ((BZ, 1, 1), (BZ, -1, 1), (BX, 1, 0), (BX, -1, 0), (BX2, 2, 0), (AX, 1), (AX, -1), (AX, 2), (AZ, 1, 0, 1), (AZ, -1, 0, 1))),
    ((DQ, 0), (), ()),
    ((DQ, 1), (), ()),
    ((DQ, 2), (), ()),
    ((DQ, 3), (), ()),
    ((DQ, 4), (), ()),
    ((DQ, 5), (), ()),
    ((DQ, 6), (), ()),
    ((DQ, 7), (), ()),
    ((COPY,), ((BZ, -1, 1),), ((BZ, -1, 2),)),
    ((COPY,), ((BZ, 1, 1),), ((BX, 1, 1), (BX, -1, 1), (BX2, 2, 1))),
    ((COPY,), (), ((BZ, 1, 2),)),
    ((DQ, 8), (), ()),
    ((COPY,), ((AZ, 1, 0, 1),), ((AZ, 1, 0, 2),)),
    ((DQ, 9), (), ()),
    ((COPY,), ((AZ, -1, 0, 1),), ((AZ, -1, 0, 2),)),
    ((COPY,), ((AX, 1), (AX, -1)), ((AZ, 1, 1, 1), (AZ, -1, 1, 1))),
    ((COPY,), ((BX, 1, 0), (BX, -1, 0), (BX2, 2, 0)), ((SHB, 0),)),
    ((COPY,), ((AX, 2),), ((SHA, 0),)),
    ((COPY,), (), ((AZ, 1, 2, 1), (AZ, -1, 2, 1))),
    ((MMA, 0, 0), (), ()),
    ((MMA, 0, 1), (), ()),
    ((MMA, 0, 2), (), ()),
    ((COPY,), ((BZ, -1, 2),), ((BZ, -1, 3),)),
    ((MMA, 0, 3), (), ()),
    ((COPY,), ((BZ, 1, 2),), ((BX, 1, 2), (BX, -1, 2), (BX2, 2, 2))),
    ((COPY,), (), ((BZ, 1, 3),)),
    ((MMA, 0, 4), (), ()),
    ((SETTLE, 5), (), ()),
    ((COPY,), ((AZ, 1, 0, 2),), ((AZ, 1, 0, 3),)),
    ((COPY,), ((AZ, -1, 0, 2),), ((AZ, -1, 0, 3),)),
    ((SETTLE, 5), (), ()),
    ((COPY,), ((BX, 1, 1), (BX, -1, 1), (BX2, 2, 1)), ((SHB, 1),)),
    ((COPY,), ((AZ, 1, 1, 1),), ((AZ, 1, 1, 2),)),
    ((COPY,), ((AZ, -1, 1, 1),), ((AZ, -1, 1, 2),)),
    ((MMB, 0, 0), ((SHA, 0), (SHB, 0)), ()),
    ((MMB, 0, 1), (), ()),
    ((MMB, 0, 2), (), ()),
    ((MMB, 0, 3), (), ()),
    ((MMB, 0, 4), (), ()),
    ((SCATTER, 0), (), ((PART, 2, 0), (PART, 1, 0), (PART, -1, 0))),
    ((COPY,), ((AZ, 1, 2, 1), (AZ, -1, 2, 1)), ((SHA, 1),)),
    ((COPY,), (), ((AZ, 1, 2, 2),)),
    ((COPY,), (), ((AZ, -1, 2, 2),)),
    ((TOT, 0), (), ()),
    ((COPY,), ((BZ, 1, 3), (BZ, -1, 3)), ((BX, 1, 3), (BX, -1, 3), (BX2, 2, 3))),
    ((COPY,), (), ((BZ4, 1),)),
    ((COPY,), (), ((BZ4, -1),)),
    ((MMA, 1, 0), (), ()),
    ((MMA, 1, 1), (), ()),
    ((MMA, 1, 2), (), ()),
    ((COPY,), ((AZ, 1, 0, 3),), ((AZ4, 1, 0),)),
    ((COPY,), ((AZ, -1, 0, 3),), ((AZ4, -1, 0),)),
    ((MMA, 1, 3), (), ()),
    ((MMA, 1, 4), (), ()),
    ((COPY,), ((BX, 1, 2), (BX, -1, 2), (BX2, 2, 2)), ((SHB, 2),)),
    ((SETTLE, 13), (), ()),
    ((COPY,), ((AZ, 1, 1, 2),), ((AZ, 1, 1, 3),)),
    ((COPY,), ((AZ, -1, 1, 2),), ((AZ, -1, 1, 3),)),
    ((SETTLE, 5), (), ()),
    ((COPY,), ((AZ, 1, 2, 2),), ((AZ, 1, 2, 3),)),
    ((COPY,), ((AZ, -1, 2, 2),), ((AZ, -1, 2, 3),)),
    ((COPY,), (), ((SHA, 2),)),
    ((MMA, 2, 0), (), ()),
    ((MMB, 1, 0), ((SHA, 1), (SHB, 1)), ()),
    ((MMB, 1, 1), (), ()),
    ((MMB, 1, 2), (), ()),
    ((MMB, 1, 3), (), ()),
    ((MMB, 1, 4), (), ()),
    ((SCATTER, 1), (), ((PART, 2, 1), (PART, 1, 1), (PART, -1, 1))),
    ((MMA, 2, 1), (), ()),
    ((COPY,), ((BZ4, 1), (BZ4, -1)), ((BX, 1, 4), (BX, -1, 4), (BX2, 2, 4))),
    ((MMA, 2, 2), (), ()),
    ((MMA, 2, 3), (), ()),
    ((COPY,), ((BX, 1, 3), (BX, -1, 3), (BX2, 2, 3)), ((SHB, 3),)),
    ((TOT, 1), (), ()),
    ((COLLECT, 0), ((PART, 1, 0), (PART, -1, 0), (PART, 2, 0)), ()),
    ((MMA, 2, 4), (), ()),
    ((COPY,), ((AZ, 1, 1, 3),), ((AZ4, 1, 1),)),
    ((COPY,), ((AZ, -1, 1, 3),), ((AZ4, -1, 1),)),
    ((SETTLE, 12), (), ()),
    ((COPY,), ((AZ, 1, 2, 3),), ((AZ4, 1, 2),)),
    ((COPY,), ((AZ, -1, 2, 3),), ((AZ4, -1, 2),)),
    ((COPY,), (), ((SHA, 3),)),
    ((MMB, 2, 0), ((SHA, 2), (SHB, 2)), ()),
    ((MMB, 2, 1), (), ()),
    ((MMB, 2, 2), (), ()),
    ((MMB, 2, 3), (), ()),
    ((MMB, 2, 4), (), ()),
    ((SCATTER, 2), (), ((PART, 2, 2), (PART, 1, 2), (PART, -1, 2))),
    ((MMA, 3, 0), (), ()),
    ((MMA, 3, 1), (), ()),
    ((TOT, 2), (), ()),
    ((MMA, 3, 2), (), ()),
    ((COPY,), ((BX, 1, 4), (BX, -1, 4), (BX2, 2, 4)), ((SHB, 4),)),
    ((MMA, 3, 3), (), ()),
    ((MMA, 3, 4), (), ()),
    ((COPY,), ((AZ4, 1, 0), (AZ4, -1, 0), (AZ4, 1, 1), (AZ4, -1, 1), (AZ4, 1, 2), (AZ4, -1, 2)), ((SHA, 4),)),
    ((MMA, 4, 0), (), ()),
    ((MMA, 4, 1), (), ()),
    ((MMA, 4, 2), (), ()),
    ((MMA, 4, 3), (), ()),
    ((MMA, 4, 4), (), ()),
    ((COLLECT, 1), ((PART, 1, 1), (PART, -1, 1), (PART, 2, 1)), ()),
    ((MMB, 3, 0), ((SHA, 3), (SHB, 3)), ()),
    ((MMB, 3, 1), (), ()),
    ((MMB, 3, 2), (), ()),
    ((MMB, 3, 3), (), ()),
    ((MMB, 3, 4), (), ()),
    ((SCATTER, 3), (), ((PART, 2, 3), (PART, 1, 3), (PART, -1, 3))),
    ((TOT, 3), (), ()),
    ((SETTLE, 10), (), ()),
    ((MMB, 4, 0), ((SHA, 4), (SHB, 4)), ()),
    ((MMB, 4, 1), (), ()),
    ((MMB, 4, 2), (), ()),
    ((MMB, 4, 3), (), ()),
    ((MMB, 4, 4), (), ()),
    ((SCATTER, 4), (), ((PART, 2, 4), (PART, 1, 4), (PART, -1, 4))),
    ((TOT, 4), (), ((TOT, 1), (TOT, -1), (TOT, 2))),
    ((SETTLE, 8), (), ()),
    ((COLLECT, 2), ((PART, 1, 2), (PART, -1, 2), (PART, 2, 2)), ()),
    ((SETTLE, 14), (), ()),
    ((COLLECT, 3), ((PART, 1, 3), (PART, -1, 3), (PART, 2, 3)), ()),
    ((SETTLE, 6), (), ()),
    ((COLLECT, 4), ((PART, 1, 4), (PART, -1, 4), (PART, 2, 4)), ()),
)


def split(v):
    hi = v.astype(bf16)
    return hi, (v - hi.astype(f32)).astype(bf16)


def dot3(a, b, dims):
    (ah, al), (bh, bl) = a, b

    def one(u, v):
        return lax.dot_general(u, v, (dims, ((), ())), preferred_element_type=f32)

    out = one(ah, bh) + one(ah, bl)
    return out if al is None else out + one(al, bh)


def precondition(q_ref, bo_ref, bi_ref, eig_ref, bd, mid, out):
    bi = bi_ref[...]
    bd[...] = jnp.zeros((128, 128), f32)
    bd[0:64, 0:64] = bi
    bd[64:128, 64:128] = bi
    even, odd = bo_ref[pl.ds(0, 32, stride=2), :], bo_ref[pl.ds(1, 32, stride=2), :]
    q = q_ref[...]
    rows = jnp.concatenate(
        [q[:, b * BLOCK : (b + 1) * BLOCK].astype(f32) for b in range(BLOCKS)], axis=0
    ).astype(bf16)
    bds = split(bd[...])
    mid[...] = dot3((rows, None), bds, ((1,), (0,)))
    t1 = jnp.concatenate([mid[pl.ds(n, BLOCKS, stride=QDEV), :] for n in range(QDEV)], axis=1)
    y = dot3(split(jnp.concatenate([even, odd], axis=1).T), split(t1), ((1,), (0,)))
    low = lax.broadcasted_iota(jnp.int32, (64, 128), 1) < 64
    eig = jnp.concatenate([eig_ref[...], eig_ref[...]], axis=1)
    parts = []
    for n in range(QDEV):
        lanes = slice(n * 128, (n + 1) * 128)
        s = jnp.where(low, y[0:64, lanes], y[64:128, lanes])
        parts.append((s + pltpu.roll(s, 64, 1)) / eig)
    u = jnp.concatenate(parts, axis=1)
    v = dot3(split(jnp.concatenate([even, odd], axis=0)), split(u), ((1,), (0,)))
    low32 = lax.broadcasted_iota(jnp.int32, (32, 128), 1) < 64
    for n in range(QDEV):
        lanes = slice(n * 128, (n + 1) * 128)
        mid[pl.ds(n, BLOCKS, stride=QDEV), :] = jnp.where(low32, v[0:32, lanes], v[32:64, lanes])
    o = dot3(split(mid[...]), bds, ((1,), (1,)))
    for b in range(BLOCKS):
        out[:, b * BLOCK : (b + 1) * BLOCK] = o[QDEV * b : QDEV * (b + 1)]


def kernel(
    q_hbm, mant_hbm, exps_hbm, bo_hbm, bi_hbm, eig_hbm, asg_hbm,
    scores_ref, totals_ref,
    q_ref, exps_ref, bo_ref, bi_ref, eig_ref, asg_ref,
    mant, w, p, acc, fac, mask, bd, mid, prep, xch,
    part_out, part_in, sums, tot, tot_in,
    ss, rs, ls, ms,
):
    e, y = lax.axis_index("ex"), lax.axis_index("lay")
    x, z, c = e // 16, (e // 2) % NZ, e % 2

    def at_x(d):
        return {"ex": (((x + d + NX) % NX) * NZ + z) * 2 + c}

    def at_z(d):
        return {"ex": (x * NZ + (z + d + NZ) % NZ) * 2 + c}

    def at_y(d):
        return {"lay": (y + d + NY) % NY}

    sibling = {"ex": (x * NZ + z) * 2 + 1 - c}

    small = [
        pltpu.make_async_copy(a, b, ls.at[i])
        for i, (a, b) in enumerate(
            (
                (q_hbm, q_ref), (bo_hbm, bo_ref), (bi_hbm, bi_ref),
                (eig_hbm, eig_ref), (exps_hbm, exps_ref), (asg_hbm, asg_ref),
            )
        )
    ]
    for cp in small:
        cp.start()
    loads = [
        pltpu.make_async_copy(
            mant_hbm.at[pl.ds(i * TCH, TCH)], mant.at[pl.ds(i * TCH, TCH)], ms.at[i]
        )
        for i in range(NCH)
    ]
    for cp in loads:
        cp.start()
    barrier = pltpu.get_barrier_semaphore()
    partners = [at_x(d) for d in (1, -1, 2)] + [at_y(d) for d in (1, -1, 2)]
    steps = {1} | {k for k in (2, 3) if k not in Z_STEP or k not in A_STEP}
    partners += [at_z(d * k) for k in sorted(steps) for d in (1, -1)] + [sibling]
    if Z_FAR or A_FAR:
        partners.append(at_z(4))
    for dev in partners:
        pl.semaphore_signal(barrier, inc=1, device_id=dev, device_id_type=MESH)

    copies, live = {}, []

    def remote(name, src, dst, dev):
        i = len(copies)
        copies[name] = pltpu.make_async_remote_copy(
            src_ref=src, dst_ref=dst, send_sem=ss.at[i], recv_sem=rs.at[i],
            device_id=dev, device_id_type=MESH,
        )

    def send(*name):
        copies[name].start()
        live.append(name)

    def arrived(*name):
        copies[name].wait_recv()

    def settle(keep=0):
        while len(live) > keep:
            copies[live.pop(0)].wait_send()

    def lanes(first, count):
        return pl.ds(pl.multiple_of(c * HALF + first, 128), count)

    la, lb, lhalf = lanes(0, KA), lanes(KA, KB), lanes(0, HALF)
    for d in (1, -1):
        hi = 0 if d == 1 else 1
        la2 = lanes(hi * (KA // 2), KA // 2)
        lb2 = lanes(KA + hi * (KB // 2), KB // 2)
        hops = [ZSLOT[(-d * k) % NZ] for k in (0, 1, 2, 3)]
        for k in (1, 2, 3):
            via = k - 1 if k in Z_STEP else 0
            remote(
                (BZ, d, k), p.at[hops[via], 0, :, lb], p.at[hops[k], 0, :, lb], at_z(d * (k - via))
            )
        if not Z_FAR:
            remote((BZ4, d), p.at[hops[3], 0, :, lb2], p.at[ZSLOT[4], 0, :, lb2], at_z(d))
        elif d == 1:
            remote((BZ4, 2), p.at[0, 0, :, lb], p.at[ZSLOT[4], 0, :, lb], at_z(4))
        for i, (first, count) in enumerate(XBLK):
            blk = pl.ds(first, count)
            for k in (1, 2, 3):
                via = k - 1 if k in A_STEP else 0
                remote(
                    (AZ, d, i, k),
                    p.at[hops[via], blk, :, la], p.at[hops[k], blk, :, la], at_z(d * (k - via)),
                )
            if not A_FAR:
                remote(
                    (AZ4, d, i), p.at[hops[3], blk, :, la2], p.at[ZSLOT[4], blk, :, la2], at_z(d)
                )
            elif d == 1:
                remote((AZ4, 2, i), p.at[0, blk, :, la], p.at[ZSLOT[4], blk, :, la], at_z(4))
        near = XSLOT[(-d) % NX]
        for i, (first, count) in enumerate(DIST):
            blk = pl.ds(first, count)
            remote((BX, d, i), p.at[blk, 0, :, lb], p.at[blk, near, :, lb], at_x(d))
            if i not in X_FAR:
                remote((BX2, d, i), p.at[blk, near, :, lb2], p.at[blk, 3, :, lb2], at_x(d))
            elif d == 1:
                remote((BX2, 2, i), p.at[blk, 0, :, lb], p.at[blk, 3, :, lb], at_x(2))
        remote((AX, d), p.at[0, 0, :, la], p.at[0, near, :, la], at_x(d))
    remote((AX, 2), p.at[0, 0, :, la], p.at[0, 3, :, la], at_x(2))
    for g, (first, count) in enumerate(GROUP):
        blk = pl.ds(first, count)
        remote((SHA, g), p.at[blk, :, :, la], p.at[blk, :, :, la], sibling)
        remote((SHB, g), p.at[blk, :, :, lb], p.at[blk, :, :, lb], sibling)
        if g in VIA:
            for i, d in enumerate((1, -1)):
                t = pl.ds(i * HT, HT)
                remote(
                    (Y2, d, g), part_out.at[2, blk, :, t], part_in.at[2, blk, :, t], at_y(d)
                )
                remote((Y1, d, g), part_out.at[i, blk], part_in.at[i, blk], at_y(d))
        else:
            for i, d in enumerate((1, -1, 2)):
                remote((PART, d, g), part_out.at[i, blk], part_in.at[i, blk], at_y(d))
    for i, d in enumerate((1, -1, 2)):
        remote((TOT, d), tot, tot_in.at[i], at_y(d))
    other_cols = pl.ds(pl.multiple_of((1 - c) * HALF, HALF), HALF)
    own_cols = pl.ds(pl.multiple_of(c * HALF, HALF), HALF)
    remote((SWAP,), prep.at[:, other_cols], xch.at[c], sibling)

    for cp in small[:4]:
        cp.wait()
    precondition(q_ref, bo_ref, bi_ref, eig_ref, bd, mid, prep)
    pl.semaphore_wait(barrier, len(partners))
    send(SWAP)
    for cp in small[4:]:
        cp.wait()
    exps = exps_ref[...]
    factor = jnp.zeros(exps.shape, f32)
    for exponent in range(lowest_exponent, highest_exponent):
        factor = factor + jnp.where(exps == exponent, f32(2.0**exponent), f32(0.0))
    fac[...] = factor
    for i in range(NX):
        one = (asg_ref[:, i * 128 : (i + 1) * 128] == 1).astype(f32)
        mask[i] = jnp.broadcast_to(one, (128, 128)).T

    def dequantize(i):
        loads[i].wait()
        t = pl.ds(i * TCH, TCH)
        for b in range(BLOCKS):
            rows = pl.ds(b * BLOCK, BLOCK)
            w[rows, t] = mant[t, rows].T * fac[b : b + 1, t].astype(bf16)

    def multiply(g, n, part):
        first, count = GROUP[g]
        blk = pl.ds(first, count)
        k = pl.ds(pl.multiple_of((c if part == 0 else 1 - c) * HALF, HALF), HALF)
        cols = pl.ds(n * NT, NT)
        rows = count * NX * PAIR
        a = p[blk, :, :, k].reshape(rows, HALF)
        if rows < 128:
            a = jnp.concatenate([a, jnp.zeros((128 - rows, HALF), bf16)], axis=0)
        r = jnp.dot(a, w[k, cols], preferred_element_type=f32)[0:rows]
        r = r.reshape(count, NX, PAIR, NT)
        acc[blk, :, :, cols] = r if part == 0 else acc[blk, :, :, cols] + r

    def slot_of(d):
        xr = (y + d + NY - x + NX) % NX
        return xr + xr // 2 - 2 * (xr // 3)

    def add_totals(g):
        t0, t1 = None, None
        first, count = GROUP[g]
        for s in range(first, first + count):
            zo = (z + ZORDER[s]) % NZ
            for j in range(NX):
                xo = (x + XORDER[j]) % NX
                m = mask[xo, pl.ds(pl.multiple_of(zo * PAIR, PAIR), PAIR), :]
                m = jnp.concatenate([m] * (ROWS // 128), axis=1)
                v = acc[s, j]
                p1 = v * m
                p0 = v - p1
                p0, p1 = p0[0:8] + p0[8:16], p1[0:8] + p1[8:16]
                t0, t1 = (p0, p1) if t0 is None else (t0 + p0, t1 + p1)
        for i, t in enumerate((t0, t1)):
            sums[i] = t if g == 0 else sums[i] + t
        if g == len(GROUP) - 1:
            tot[...] = jnp.zeros(tot.shape, f32)
            for i in range(2):
                total = jnp.sum(sums[i], axis=0, keepdims=True)
                for n in range(ROWS // NT):
                    tot[8 * i + n : 8 * i + n + 1, :] = total[:, n * NT : (n + 1) * NT]

    def scatter(g):
        first, count = GROUP[g]
        for i, d in ((2, 2),) if g in VIA else ((2, 2), (0, 1), (1, -1)):
            to = slot_of(d)
            for s in range(first, first + count):
                part_out[i, s] = acc[s, to].astype(bf16)

    def combine(g):
        first, count = GROUP[g]
        for i, d in ((0, 1), (1, -1)):
            to = slot_of(d)
            for j in range(2):
                t = pl.ds(j * HT, HT)
                for s in range(first, first + count):
                    v = acc[s, to, :, t]
                    v = v + part_in[2, s, :, t].astype(f32) if i == j else v
                    part_out[i, s, :, t] = v.astype(bf16)

    normalizer = 1.0 / math.sqrt(NY * ENTRIES)

    def collect(g):
        mine = slot_of(0)
        first, count = GROUP[g]
        for s in range(first, first + count):
            total = acc[s, mine] + part_in[0, s].astype(f32)
            total = total + part_in[1, s].astype(f32)
            if g not in VIA:
                total = total + part_in[2, s].astype(f32)
            zo = (z + ZORDER[s]) % NZ
            scores_ref[pl.ds(pl.multiple_of(zo * PAIR, PAIR), PAIR), :] = total * normalizer

    do = {
        COPY: lambda: None, SETTLE: lambda n: settle(max(len(live) - n, 0)),
        DQ: lambda i: None if i < EARLY else dequantize(i),
        MMA: lambda g, n: multiply(g, n, 0), MMB: lambda g, n: multiply(g, n, 1),
        SCATTER: scatter, COMB: combine, TOT: add_totals, COLLECT: collect,
    }
    xch[c] = prep[:, own_cols]
    for i in range(EARLY):
        dequantize(i)
    arrived(SWAP)
    p[0, 0, :, lhalf] = xch[...].reshape(PAIR, HALF).astype(bf16)
    for i, ((step, *args), waits, sends) in enumerate(STEPS):
        if i == len(STEPS) - 1:
            settle(6)
        for name in waits:
            arrived(*name)
        do[step](*args)
        for name in sends:
            send(*name)
    for d in (1, -1, 2):
        arrived(TOT, d)
    total = tot[...] + tot_in[0] + tot_in[1] + tot_in[2]
    for i in range(2):
        for n in range(ROWS // NT):
            row = total[8 * i + n : 8 * i + n + 1, :]
            totals_ref[i : i + 1, n * NT : (n + 1) * NT] = row * (normalizer / math.sqrt(QB))
    settle()


N_COPIES = 2 * (3 + 1 + 4 * len(XBLK) + 10 + 1) - len(X_FAR) - Z_FAR - A_FAR * len(XBLK) + 1 + 5 * len(GROUP) + len(VIA) + 3 + 1


def body(queries, train_mantissa, scale_exponents, basis_out, basis_in, eigen, assignment):
    hbm = pl.BlockSpec(memory_space=pl.ANY)
    vmem = pltpu.VMEM
    dma = pltpu.SemaphoreType.DMA
    piece = (3, NZ, PAIR, ROWS)
    scores, totals = pl.pallas_call(
        kernel,
        out_shape=(
            pltpu.VMEM((NX * 32, ROWS), f32),
            pltpu.VMEM((2, ROWS), f32),
        ),
        in_specs=[hbm] * 7,
        out_specs=(pl.BlockSpec(memory_space=pltpu.VMEM),) * 2,
        scratch_shapes=[
            vmem((QDEV, ENTRIES), bf16),
            vmem((BLOCKS, ROWS), jnp.int32),
            vmem((ORDER, ORDER), f32),
            vmem((ORDER, ORDER), f32),
            vmem((ORDER, ORDER), f32),
            vmem((1, 512), jnp.int32),
            vmem((ROWS, ENTRIES), bf16),
            vmem((ENTRIES, ROWS), bf16),
            vmem((NZ, NX, PAIR, ENTRIES), bf16),
            vmem((NZ, NX, PAIR, ROWS), f32),
            vmem((BLOCKS, ROWS), f32),
            vmem((NX, 128, 128), f32),
            vmem((128, 128), f32),
            vmem((BLOCKS * QDEV, 128), f32),
            vmem((QDEV, ENTRIES), f32),
            vmem((2, QDEV, HALF), f32),
            vmem(piece, bf16),
            vmem(piece, bf16),
            vmem((2, 8, ROWS), f32),
            vmem((16, NT), f32),
            vmem((3, 16, NT), f32),
            dma((N_COPIES,)),
            dma((N_COPIES,)),
            dma((6,)),
            dma((NCH,)),
        ],
        compiler_params=pltpu.CompilerParams(
            collective_id=0, has_side_effects=True, vmem_limit_bytes=56 * 2**20
        ),
        name="influence",
    )(
        queries.reshape(QDEV, ENTRIES),
        train_mantissa.reshape(ROWS, ENTRIES),
        scale_exponents.reshape(ROWS, BLOCKS).T,
        basis_out.reshape(ORDER, ORDER),
        basis_in.reshape(ORDER, ORDER),
        eigen.reshape(ORDER, ORDER),
        assignment.reshape(1, 512),
    )
    return scores, totals


def solution(mesh):
    placed = (
        P("ex", "lay", None),
        P("ex", "lay", None),
        P("ex", "lay", None),
        P("lay", None, None),
        P("lay", None, None),
        P("lay", None, None),
        P(),
    )
    return jax.shard_map(
        body, mesh=mesh, in_specs=placed, out_specs=(P("lay", "ex"), P(None, "ex")), check_vma=False
    )
```

```python
import math

import jax
import jax.numpy as jnp
from jax import lax
from jax.experimental import pallas as pl
from jax.experimental.pallas import tpu as pltpu
from jax.sharding import PartitionSpec as P

MESH = pl.DeviceIdType.MESH
f32, bf16 = jnp.float32, jnp.bfloat16

NX, NY, NZ = 4, 4, 8
ORDER = 64
ENTRIES = ORDER * ORDER
HALF = ENTRIES // 2
BLOCKS = 32
BLOCK = ENTRIES // BLOCKS
ROWS = 1280
QDEV = 8
PAIR = 16
KA = 768
KB = HALF - KA
NT = 256
HT = ROWS // 2
TCH = 128
NCH = ROWS // TCH
EARLY = 2
(
    COPY, SETTLE, DQ, MMA, MMB, SCATTER, COMB, TOT, COLLECT,
    BZ, BZ4, BX, BX2, AX, AZ, AZ4, SHA, SHB, PART, Y1, Y2, SWAP,
) = range(22)
QB = 256
lowest_exponent = -2
highest_exponent = 2

ZORDER = (0, 1, 7, 2, 6, 3, 5, 4)
ZSLOT = {zr: i for i, zr in enumerate(ZORDER)}
XORDER = (0, 1, 3, 2)
XSLOT = {xr: i for i, xr in enumerate(XORDER)}
XBLK = ((0, 1), (1, 2), (3, 1))
DIST = ((0, 1), (1, 2), (3, 2), (5, 2), (7, 1))
GROUP = ((0, 1), (1, 2), (3, 2), (5, 2), (7, 1))
Z_STEP = (3,)
A_STEP = (2, 3)
X_FAR = (0, 1, 2, 3, 4)
Z_FAR, A_FAR = (0, 0)
VIA = ()
STEPS = (
    ((COPY,), (), ((BZ, 1, 1), (BZ, -1, 1), (BX, 1, 0), (BX, -1, 0), (BX2, 2, 0), (AX, 1), (AX, -1), (AX, 2), (BZ, 1, 2), (BZ, -1, 2), (AZ, 1, 0, 1), (AZ, -1, 0, 1))),
    ((COPY,), (), ((SHB, 0, 0),)),
    ((COPY,), (), ((SHA, 0, 0),)),
    ((DQ, 0), (), ()),
    ((DQ, 1), (), ()),
    ((DQ, 2), (), ()),
    ((DQ, 3), (), ()),
    ((DQ, 4), (), ()),
    ((DQ, 5), (), ()),
    ((DQ, 6), (), ()),
    ((DQ, 7), (), ()),
    ((COPY,), ((BZ, 1, 1), (BZ, -1, 1)), ((BX, 1, 1), (BX, -1, 1), (BX2, 2, 1))),
    ((COPY,), ((BX, 1, 0), (BX, -1, 0)), ((SHB, 0, 1),)),
    ((DQ, 8), (), ()),
    ((DQ, 9), (), ()),
    ((COPY,), ((AX, 1), (AX, -1)), ((AZ, 1, 1, 1), (AZ, -1, 1, 1))),
    ((COPY,), (), ((SHA, 0, 1),)),
    ((COPY,), (), ((SHB, 1, 0),)),
    ((COPY,), ((AZ, 1, 0, 1),), ((AZ, 1, 0, 2),)),
    ((COPY,), ((AZ, -1, 0, 1),), ((SHA, 1, 0),)),
    ((COPY,), (), ((AZ, -1, 0, 2),)),
    ((COPY,), ((BX2, 2, 0),), ((SHB, 0, 2),)),
    ((COPY,), ((AX, 2),), ((SHA, 0, 2),)),
    ((COPY,), (), ((AZ, 1, 2, 1), (AZ, -1, 2, 1))),
    ((MMA, 0, 0), (), ()),
    ((COPY,), ((BZ, -1, 2),), ((BZ, -1, 3),)),
    ((COPY,), ((BZ, 1, 2),), ((SHB, 2, 0),)),
    ((MMA, 0, 1), (), ()),
    ((COPY,), (), ((BZ, 1, 3),)),
    ((COPY,), (), ((BX, 1, 2), (BX, -1, 2), (BX2, 2, 2))),
    ((MMA, 0, 2), (), ()),
    ((MMA, 0, 3), (), ()),
    ((MMA, 0, 4), (), ()),
    ((SETTLE, 14), (), ()),
    ((COPY,), ((BX, 1, 1), (BX, -1, 1)), ((SHB, 1, 1),)),
    ((COPY,), ((AZ, 1, 1, 1),), ((AZ, 1, 1, 2),)),
    ((COPY,), ((AZ, -1, 1, 1),), ((SHA, 1, 1),)),
    ((COPY,), (), ((AZ, -1, 1, 2),)),
    ((MMB, 0, 0), ((SHA, 0, 0), (SHA, 0, 1), (SHA, 0, 2), (SHB, 0, 0), (SHB, 0, 1), (SHB, 0, 2)), ()),
    ((COPY,), ((AZ, -1, 0, 2),), ((AZ, -1, 0, 3),)),
    ((COPY,), ((AZ, 1, 0, 2),), ((SHA, 2, 0),)),
    ((COPY,), (), ((AZ, 1, 0, 3),)),
    ((MMB, 0, 1), (), ()),
    ((MMB, 0, 2), (), ()),
    ((COPY,), ((AZ, 1, 2, 1),), ((AZ, 1, 2, 2),)),
    ((COPY,), ((AZ, -1, 2, 1),), ((SHA, 1, 2),)),
    ((COPY,), (), ((AZ, -1, 2, 2),)),
    ((MMB, 0, 3), (), ()),
    ((MMB, 0, 4), (), ()),
    ((COPY,), ((BX2, 2, 1),), ((SHB, 1, 2),)),
    ((SCATTER, 0), (), ((PART, 2, 0), (PART, 1, 0), (PART, -1, 0))),
    ((COPY,), ((BZ, 1, 3),), ((BZ4, 1),)),
    ((COPY,), ((BZ, -1, 3),), ((BZ4, -1),)),
    ((TOT, 0), (), ()),
    ((COPY,), (), ((SHB, 3, 0),)),
    ((COPY,), (), ((BX, 1, 3), (BX, -1, 3), (BX2, 2, 3))),
    ((MMA, 1, 0), (), ()),
    ((MMA, 1, 1), (), ()),
    ((MMA, 1, 2), (), ()),
    ((MMA, 1, 3), (), ()),
    ((MMA, 1, 4), (), ()),
    ((COPY,), ((AZ, -1, 1, 2),), ((AZ, -1, 1, 3),)),
    ((COPY,), ((AZ, 1, 1, 2),), ((SHA, 2, 1),)),
    ((COPY,), (), ((AZ, 1, 1, 3),)),
    ((COPY,), ((BX, 1, 2), (BX, -1, 2)), ((SHB, 2, 1),)),
    ((COPY,), ((AZ, 1, 0, 3),), ((AZ4, 1, 0),)),
    ((COPY,), ((AZ, -1, 0, 3),), ((SHA, 3, 0),)),
    ((COPY,), (), ((AZ4, -1, 0),)),
    ((SETTLE, 8), (), ()),
    ((COPY,), ((AZ, 1, 2, 2),), ((AZ, 1, 2, 3),)),
    ((COPY,), ((AZ, -1, 2, 2),), ((AZ, -1, 2, 3),)),
    ((COPY,), (), ((SHA, 2, 2),)),
    ((MMB, 1, 0), ((SHA, 1, 0), (SHA, 1, 1), (SHA, 1, 2), (SHB, 1, 0), (SHB, 1, 1), (SHB, 1, 2)), ()),
    ((MMB, 1, 1), (), ()),
    ((MMB, 1, 2), (), ()),
    ((MMB, 1, 3), (), ()),
    ((MMB, 1, 4), (), ()),
    ((COPY,), ((BX2, 2, 2),), ((SHB, 2, 2),)),
    ((SCATTER, 1), (), ((PART, 2, 1), (PART, 1, 1), (PART, -1, 1))),
    ((COPY,), ((BZ4, 1), (BZ4, -1)), ((SHB, 4, 0),)),
    ((COLLECT, 0), ((PART, 1, 0), (PART, -1, 0), (PART, 2, 0)), ()),
    ((COPY,), (), ((BX, 1, 4), (BX, -1, 4), (BX2, 2, 4))),
    ((MMA, 2, 0), (), ()),
    ((MMA, 2, 1), (), ()),
    ((MMA, 2, 2), (), ()),
    ((COPY,), ((AZ, 1, 1, 3), (AZ, -1, 1, 3)), ((SHA, 3, 1),)),
    ((COPY,), (), ((AZ4, -1, 1),)),
    ((COPY,), (), ((AZ4, 1, 1),)),
    ((COPY,), ((AZ4, 1, 0), (AZ4, -1, 0)), ((SHA, 4, 0),)),
    ((MMA, 2, 3), (), ()),
    ((MMA, 2, 4), (), ()),
    ((TOT, 1), (), ()),
    ((COPY,), ((AZ, 1, 2, 3), (AZ, -1, 2, 3)), ((SHA, 3, 2),)),
    ((COPY,), (), ((AZ4, -1, 2),)),
    ((COPY,), (), ((AZ4, 1, 2),)),
    ((COPY,), ((BX, 1, 3), (BX, -1, 3)), ((SHB, 3, 1),)),
    ((SETTLE, 9), (), ()),
    ((MMB, 2, 0), ((SHA, 2, 0), (SHA, 2, 1), (SHA, 2, 2), (SHB, 2, 0), (SHB, 2, 1), (SHB, 2, 2)), ()),
    ((MMB, 2, 1), (), ()),
    ((MMB, 2, 2), (), ()),
    ((MMB, 2, 3), (), ()),
    ((MMB, 2, 4), (), ()),
    ((SCATTER, 2), (), ((PART, 2, 2), (PART, 1, 2), (PART, -1, 2))),
    ((COPY,), ((BX2, 2, 3),), ((SHB, 3, 2),)),
    ((MMA, 3, 0), (), ()),
    ((MMA, 3, 1), (), ()),
    ((MMA, 3, 2), (), ()),
    ((COPY,), ((AZ4, 1, 2), (AZ4, -1, 2)), ((SHA, 4, 2),)),
    ((MMA, 3, 3), (), ()),
    ((MMA, 3, 4), (), ()),
    ((COPY,), ((BX, 1, 4), (BX, -1, 4)), ((SHB, 4, 1),)),
    ((COPY,), ((AZ4, 1, 1), (AZ4, -1, 1)), ((SHA, 4, 1),)),
    ((TOT, 2), (), ()),
    ((SETTLE, 11), (), ()),
    ((COPY,), ((BX2, 2, 4),), ((SHB, 4, 2),)),
    ((MMA, 4, 0), (), ()),
    ((MMA, 4, 1), (), ()),
    ((MMA, 4, 2), (), ()),
    ((MMA, 4, 3), (), ()),
    ((MMA, 4, 4), (), ()),
    ((MMB, 3, 0), ((SHA, 3, 0), (SHA, 3, 1), (SHA, 3, 2), (SHB, 3, 0), (SHB, 3, 1), (SHB, 3, 2)), ()),
    ((MMB, 3, 1), (), ()),
    ((MMB, 3, 2), (), ()),
    ((MMB, 3, 3), (), ()),
    ((MMB, 3, 4), (), ()),
    ((SCATTER, 3), (), ((PART, 2, 3), (PART, 1, 3), (PART, -1, 3))),
    ((TOT, 3), (), ()),
    ((COLLECT, 1), ((PART, 1, 1), (PART, -1, 1), (PART, 2, 1)), ()),
    ((MMB, 4, 0), ((SHA, 4, 0), (SHA, 4, 1), (SHA, 4, 2), (SHB, 4, 0), (SHB, 4, 1), (SHB, 4, 2)), ()),
    ((MMB, 4, 1), (), ()),
    ((MMB, 4, 2), (), ()),
    ((MMB, 4, 3), (), ()),
    ((MMB, 4, 4), (), ()),
    ((SCATTER, 4), (), ((PART, 2, 4), (PART, 1, 4), (PART, -1, 4))),
    ((TOT, 4), (), ((TOT, 1), (TOT, -1), (TOT, 2))),
    ((COLLECT, 2), ((PART, 1, 2), (PART, -1, 2), (PART, 2, 2)), ()),
    ((SETTLE, 47), (), ()),
    ((COLLECT, 3), ((PART, 1, 3), (PART, -1, 3), (PART, 2, 3)), ()),
    ((SETTLE, 9), (), ()),
    ((COLLECT, 4), ((PART, 1, 4), (PART, -1, 4), (PART, 2, 4)), ()),
)


def split(v):
    hi = v.astype(bf16)
    return hi, (v - hi.astype(f32)).astype(bf16)


def dot3(a, b, dims):
    (ah, al), (bh, bl) = a, b

    def one(u, v):
        return lax.dot_general(u, v, (dims, ((), ())), preferred_element_type=f32)

    out = one(ah, bh) + one(ah, bl)
    return out if al is None else out + one(al, bh)


def precondition(q_ref, bo_ref, bi_ref, eig_ref, bd, mid, out):
    bi = bi_ref[...]
    bd[...] = jnp.zeros((128, 128), f32)
    bd[0:64, 0:64] = bi
    bd[64:128, 64:128] = bi
    even, odd = bo_ref[pl.ds(0, 32, stride=2), :], bo_ref[pl.ds(1, 32, stride=2), :]
    q = q_ref[...]
    rows = jnp.concatenate(
        [q[:, b * BLOCK : (b + 1) * BLOCK].astype(f32) for b in range(BLOCKS)], axis=0
    ).astype(bf16)
    bds = split(bd[...])
    mid[...] = dot3((rows, None), bds, ((1,), (0,)))
    t1 = jnp.concatenate([mid[pl.ds(n, BLOCKS, stride=QDEV), :] for n in range(QDEV)], axis=1)
    y = dot3(split(jnp.concatenate([even, odd], axis=1).T), split(t1), ((1,), (0,)))
    low = lax.broadcasted_iota(jnp.int32, (64, 128), 1) < 64
    eig = jnp.concatenate([eig_ref[...], eig_ref[...]], axis=1)
    parts = []
    for n in range(QDEV):
        lanes = slice(n * 128, (n + 1) * 128)
        s = jnp.where(low, y[0:64, lanes], y[64:128, lanes])
        parts.append((s + pltpu.roll(s, 64, 1)) / eig)
    u = jnp.concatenate(parts, axis=1)
    v = dot3(split(jnp.concatenate([even, odd], axis=0)), split(u), ((1,), (0,)))
    low32 = lax.broadcasted_iota(jnp.int32, (32, 128), 1) < 64
    for n in range(QDEV):
        lanes = slice(n * 128, (n + 1) * 128)
        mid[pl.ds(n, BLOCKS, stride=QDEV), :] = jnp.where(low32, v[0:32, lanes], v[32:64, lanes])
    o = dot3(split(mid[...]), bds, ((1,), (1,)))
    for b in range(BLOCKS):
        out[:, b * BLOCK : (b + 1) * BLOCK] = o[QDEV * b : QDEV * (b + 1)]


def kernel(
    q_hbm, mant_hbm, exps_hbm, bo_hbm, bi_hbm, eig_hbm, asg_hbm,
    scores_ref, totals_ref,
    q_ref, exps_ref, bo_ref, bi_ref, eig_ref, asg_ref,
    mant, w, p, acc, fac, mask, bd, mid, prep, xch,
    part_out, part_in, sums, tot, tot_in,
    ss, rs, ls, ms,
):
    e, y = lax.axis_index("ex"), lax.axis_index("lay")
    x, z, c = e // 16, (e // 2) % NZ, e % 2

    def at_x(d):
        return {"ex": (((x + d + NX) % NX) * NZ + z) * 2 + c}

    def at_z(d):
        return {"ex": (x * NZ + (z + d + NZ) % NZ) * 2 + c}

    def at_y(d):
        return {"lay": (y + d + NY) % NY}

    sibling = {"ex": (x * NZ + z) * 2 + 1 - c}

    small = [
        pltpu.make_async_copy(a, b, ls.at[i])
        for i, (a, b) in enumerate(
            (
                (q_hbm, q_ref), (bo_hbm, bo_ref), (bi_hbm, bi_ref),
                (eig_hbm, eig_ref), (exps_hbm, exps_ref), (asg_hbm, asg_ref),
            )
        )
    ]
    for cp in small:
        cp.start()
    loads = [
        pltpu.make_async_copy(
            mant_hbm.at[pl.ds(i * TCH, TCH)], mant.at[pl.ds(i * TCH, TCH)], ms.at[i]
        )
        for i in range(NCH)
    ]
    for cp in loads:
        cp.start()
    barrier = pltpu.get_barrier_semaphore()
    partners = [at_x(d) for d in (1, -1, 2)] + [at_y(d) for d in (1, -1, 2)]
    steps = {1} | {k for k in (2, 3) if k not in Z_STEP or k not in A_STEP}
    partners += [at_z(d * k) for k in sorted(steps) for d in (1, -1)] + [sibling]
    if Z_FAR or A_FAR:
        partners.append(at_z(4))
    for dev in partners:
        pl.semaphore_signal(barrier, inc=1, device_id=dev, device_id_type=MESH)

    copies, live = {}, []

    def remote(name, src, dst, dev):
        i = len(copies)
        copies[name] = pltpu.make_async_remote_copy(
            src_ref=src, dst_ref=dst, send_sem=ss.at[i], recv_sem=rs.at[i],
            device_id=dev, device_id_type=MESH,
        )

    def send(*name):
        copies[name].start()
        live.append(name)

    def arrived(*name):
        copies[name].wait_recv()

    def settle(keep=0):
        while len(live) > keep:
            copies[live.pop(0)].wait_send()

    def lanes(first, count):
        return pl.ds(pl.multiple_of(c * HALF + first, 128), count)

    la, lb, lhalf = lanes(0, KA), lanes(KA, KB), lanes(0, HALF)
    for d in (1, -1):
        hi = 0 if d == 1 else 1
        la2 = lanes(hi * (KA // 2), KA // 2)
        lb2 = lanes(KA + hi * (KB // 2), KB // 2)
        hops = [ZSLOT[(-d * k) % NZ] for k in (0, 1, 2, 3)]
        for k in (1, 2, 3):
            via = k - 1 if k in Z_STEP else 0
            remote(
                (BZ, d, k), p.at[hops[via], 0, :, lb], p.at[hops[k], 0, :, lb], at_z(d * (k - via))
            )
        if not Z_FAR:
            remote((BZ4, d), p.at[hops[3], 0, :, lb2], p.at[ZSLOT[4], 0, :, lb2], at_z(d))
        elif d == 1:
            remote((BZ4, 2), p.at[0, 0, :, lb], p.at[ZSLOT[4], 0, :, lb], at_z(4))
        for i, (first, count) in enumerate(XBLK):
            blk = pl.ds(first, count)
            for k in (1, 2, 3):
                via = k - 1 if k in A_STEP else 0
                remote(
                    (AZ, d, i, k),
                    p.at[hops[via], blk, :, la], p.at[hops[k], blk, :, la], at_z(d * (k - via)),
                )
            if not A_FAR:
                remote(
                    (AZ4, d, i), p.at[hops[3], blk, :, la2], p.at[ZSLOT[4], blk, :, la2], at_z(d)
                )
            elif d == 1:
                remote((AZ4, 2, i), p.at[0, blk, :, la], p.at[ZSLOT[4], blk, :, la], at_z(4))
        near = XSLOT[(-d) % NX]
        for i, (first, count) in enumerate(DIST):
            blk = pl.ds(first, count)
            remote((BX, d, i), p.at[blk, 0, :, lb], p.at[blk, near, :, lb], at_x(d))
            if i not in X_FAR:
                remote((BX2, d, i), p.at[blk, near, :, lb2], p.at[blk, 3, :, lb2], at_x(d))
            elif d == 1:
                remote((BX2, 2, i), p.at[blk, 0, :, lb], p.at[blk, 3, :, lb], at_x(2))
        remote((AX, d), p.at[0, 0, :, la], p.at[0, near, :, la], at_x(d))
    remote((AX, 2), p.at[0, 0, :, la], p.at[0, 3, :, la], at_x(2))
    for g, (first, count) in enumerate(GROUP):
        blk = pl.ds(first, count)
        for k, (low, wide) in enumerate(XBLK):
            xs = pl.ds(low, wide)
            remote((SHA, g, k), p.at[blk, xs, :, la], p.at[blk, xs, :, la], sibling)
            remote((SHB, g, k), p.at[blk, xs, :, lb], p.at[blk, xs, :, lb], sibling)
        if g in VIA:
            for i, d in enumerate((1, -1)):
                t = pl.ds(i * HT, HT)
                remote(
                    (Y2, d, g), part_out.at[2, blk, :, t], part_in.at[2, blk, :, t], at_y(d)
                )
                remote((Y1, d, g), part_out.at[i, blk], part_in.at[i, blk], at_y(d))
        else:
            for i, d in enumerate((1, -1, 2)):
                remote((PART, d, g), part_out.at[i, blk], part_in.at[i, blk], at_y(d))
    for i, d in enumerate((1, -1, 2)):
        remote((TOT, d), tot, tot_in.at[i], at_y(d))
    other_cols = pl.ds(pl.multiple_of((1 - c) * HALF, HALF), HALF)
    own_cols = pl.ds(pl.multiple_of(c * HALF, HALF), HALF)
    remote((SWAP,), prep.at[:, other_cols], xch.at[c], sibling)

    for cp in small[:4]:
        cp.wait()
    precondition(q_ref, bo_ref, bi_ref, eig_ref, bd, mid, prep)
    pl.semaphore_wait(barrier, len(partners))
    send(SWAP)
    for cp in small[4:]:
        cp.wait()
    exps = exps_ref[...]
    factor = jnp.zeros(exps.shape, f32)
    for exponent in range(lowest_exponent, highest_exponent):
        factor = factor + jnp.where(exps == exponent, f32(2.0**exponent), f32(0.0))
    fac[...] = factor
    for i in range(NX):
        one = (asg_ref[:, i * 128 : (i + 1) * 128] == 1).astype(f32)
        mask[i] = jnp.broadcast_to(one, (128, 128)).T

    def dequantize(i):
        loads[i].wait()
        t = pl.ds(i * TCH, TCH)
        for b in range(BLOCKS):
            rows = pl.ds(b * BLOCK, BLOCK)
            w[rows, t] = mant[t, rows].T * fac[b : b + 1, t].astype(bf16)

    def multiply(g, n, part):
        first, count = GROUP[g]
        blk = pl.ds(first, count)
        k = pl.ds(pl.multiple_of((c if part == 0 else 1 - c) * HALF, HALF), HALF)
        cols = pl.ds(n * NT, NT)
        rows = count * NX * PAIR
        a = p[blk, :, :, k].reshape(rows, HALF)
        if rows < 128:
            a = jnp.concatenate([a, jnp.zeros((128 - rows, HALF), bf16)], axis=0)
        r = jnp.dot(a, w[k, cols], preferred_element_type=f32)[0:rows]
        r = r.reshape(count, NX, PAIR, NT)
        acc[blk, :, :, cols] = r if part == 0 else acc[blk, :, :, cols] + r

    def slot_of(d):
        xr = (y + d + NY - x + NX) % NX
        return xr + xr // 2 - 2 * (xr // 3)

    def add_totals(g):
        t0, t1 = None, None
        first, count = GROUP[g]
        for s in range(first, first + count):
            zo = (z + ZORDER[s]) % NZ
            for j in range(NX):
                xo = (x + XORDER[j]) % NX
                m = mask[xo, pl.ds(pl.multiple_of(zo * PAIR, PAIR), PAIR), :]
                m = jnp.concatenate([m] * (ROWS // 128), axis=1)
                v = acc[s, j]
                p1 = v * m
                p0 = v - p1
                p0, p1 = p0[0:8] + p0[8:16], p1[0:8] + p1[8:16]
                t0, t1 = (p0, p1) if t0 is None else (t0 + p0, t1 + p1)
        for i, t in enumerate((t0, t1)):
            sums[i] = t if g == 0 else sums[i] + t
        if g == len(GROUP) - 1:
            tot[...] = jnp.zeros(tot.shape, f32)
            for i in range(2):
                total = jnp.sum(sums[i], axis=0, keepdims=True)
                for n in range(ROWS // NT):
                    tot[8 * i + n : 8 * i + n + 1, :] = total[:, n * NT : (n + 1) * NT]

    def scatter(g):
        first, count = GROUP[g]
        for i, d in ((2, 2),) if g in VIA else ((2, 2), (0, 1), (1, -1)):
            to = slot_of(d)
            for s in range(first, first + count):
                part_out[i, s] = acc[s, to].astype(bf16)

    def combine(g):
        first, count = GROUP[g]
        for i, d in ((0, 1), (1, -1)):
            to = slot_of(d)
            for j in range(2):
                t = pl.ds(j * HT, HT)
                for s in range(first, first + count):
                    v = acc[s, to, :, t]
                    v = v + part_in[2, s, :, t].astype(f32) if i == j else v
                    part_out[i, s, :, t] = v.astype(bf16)

    normalizer = 1.0 / math.sqrt(NY * ENTRIES)

    def collect(g):
        mine = slot_of(0)
        first, count = GROUP[g]
        for s in range(first, first + count):
            total = acc[s, mine] + part_in[0, s].astype(f32)
            total = total + part_in[1, s].astype(f32)
            if g not in VIA:
                total = total + part_in[2, s].astype(f32)
            zo = (z + ZORDER[s]) % NZ
            scores_ref[pl.ds(pl.multiple_of(zo * PAIR, PAIR), PAIR), :] = total * normalizer

    do = {
        COPY: lambda: None, SETTLE: lambda n: settle(max(len(live) - n, 0)),
        DQ: lambda i: None if i < EARLY else dequantize(i),
        MMA: lambda g, n: multiply(g, n, 0), MMB: lambda g, n: multiply(g, n, 1),
        SCATTER: scatter, COMB: combine, TOT: add_totals, COLLECT: collect,
    }
    xch[c] = prep[:, own_cols]
    for i in range(EARLY):
        dequantize(i)
    arrived(SWAP)
    p[0, 0, :, lhalf] = xch[...].reshape(PAIR, HALF).astype(bf16)
    for i, ((step, *args), waits, sends) in enumerate(STEPS):
        if i == len(STEPS) - 1:
            settle(6)
        for name in waits:
            arrived(*name)
        do[step](*args)
        for name in sends:
            send(*name)
    for d in (1, -1, 2):
        arrived(TOT, d)
    total = tot[...] + tot_in[0] + tot_in[1] + tot_in[2]
    for i in range(2):
        for n in range(ROWS // NT):
            row = total[8 * i + n : 8 * i + n + 1, :]
            totals_ref[i : i + 1, n * NT : (n + 1) * NT] = row * (normalizer / math.sqrt(QB))
    settle()


N_COPIES = 2 * (3 + 1 + 4 * len(XBLK) + 10 + 1) - len(X_FAR) - Z_FAR - A_FAR * len(XBLK) + 1 + 9 * len(GROUP) + len(VIA) + 3 + 1


def body(queries, train_mantissa, scale_exponents, basis_out, basis_in, eigen, assignment):
    hbm = pl.BlockSpec(memory_space=pl.ANY)
    vmem = pltpu.VMEM
    dma = pltpu.SemaphoreType.DMA
    piece = (3, NZ, PAIR, ROWS)
    scores, totals = pl.pallas_call(
        kernel,
        out_shape=(
            pltpu.VMEM((NX * 32, ROWS), f32),
            pltpu.VMEM((2, ROWS), f32),
        ),
        in_specs=[hbm] * 7,
        out_specs=(pl.BlockSpec(memory_space=pltpu.VMEM),) * 2,
        scratch_shapes=[
            vmem((QDEV, ENTRIES), bf16),
            vmem((BLOCKS, ROWS), jnp.int32),
            vmem((ORDER, ORDER), f32),
            vmem((ORDER, ORDER), f32),
            vmem((ORDER, ORDER), f32),
            vmem((1, 512), jnp.int32),
            vmem((ROWS, ENTRIES), bf16),
            vmem((ENTRIES, ROWS), bf16),
            vmem((NZ, NX, PAIR, ENTRIES), bf16),
            vmem((NZ, NX, PAIR, ROWS), f32),
            vmem((BLOCKS, ROWS), f32),
            vmem((NX, 128, 128), f32),
            vmem((128, 128), f32),
            vmem((BLOCKS * QDEV, 128), f32),
            vmem((QDEV, ENTRIES), f32),
            vmem((2, QDEV, HALF), f32),
            vmem(piece, bf16),
            vmem(piece, bf16),
            vmem((2, 8, ROWS), f32),
            vmem((16, NT), f32),
            vmem((3, 16, NT), f32),
            dma((N_COPIES,)),
            dma((N_COPIES,)),
            dma((6,)),
            dma((NCH,)),
        ],
        compiler_params=pltpu.CompilerParams(
            collective_id=0, has_side_effects=True, vmem_limit_bytes=56 * 2**20
        ),
        name="influence",
    )(
        queries.reshape(QDEV, ENTRIES),
        train_mantissa.reshape(ROWS, ENTRIES),
        scale_exponents.reshape(ROWS, BLOCKS).T,
        basis_out.reshape(ORDER, ORDER),
        basis_in.reshape(ORDER, ORDER),
        eigen.reshape(ORDER, ORDER),
        assignment.reshape(1, 512),
    )
    return scores, totals


def solution(mesh):
    placed = (
        P("ex", "lay", None),
        P("ex", "lay", None),
        P("ex", "lay", None),
        P("lay", None, None),
        P("lay", None, None),
        P("lay", None, None),
        P(),
    )
    return jax.shard_map(
        body, mesh=mesh, in_specs=placed, out_specs=(P("lay", "ex"), P(None, "ex")), check_vma=False
    )
```

```python
import math

import jax
import jax.numpy as jnp
from jax import lax
from jax.experimental import pallas as pl
from jax.experimental.pallas import tpu as pltpu
from jax.sharding import PartitionSpec as P

MESH = pl.DeviceIdType.MESH
f32, bf16 = jnp.float32, jnp.bfloat16

NX, NY, NZ = 4, 4, 8
ORDER = 64
ENTRIES = ORDER * ORDER
HALF = ENTRIES // 2
BLOCKS = 32
BLOCK = ENTRIES // BLOCKS
ROWS = 1280
QDEV = 8
PAIR = 16
KA = 1024
KB = HALF - KA
NT = 256
HT = ROWS // 2
TCH = 128
NCH = ROWS // TCH
EARLY = 1
(
    COPY, SETTLE, DQ, MMA, MMB, SCATTER, COMB, TOT, COLLECT,
    BZ, BZ4, BX, BX2, AX, AZ, AZ4, SHA, SHB, PART, Y1, Y2, SWAP,
) = range(22)
QB = 256
lowest_exponent = -2
highest_exponent = 2

ZORDER = (0, 1, 7, 2, 6, 3, 5, 4)
ZSLOT = {zr: i for i, zr in enumerate(ZORDER)}
XORDER = (0, 1, 3, 2)
XSLOT = {xr: i for i, xr in enumerate(XORDER)}
XBLK = ((0, 1), (1, 2), (3, 1))
DIST = ((0, 1), (1, 2), (3, 2), (5, 2), (7, 1))
GROUP = ((0, 1), (1, 2), (3, 2), (5, 2), (7, 1))
Z_STEP = (2, 3)
A_STEP = (2, 3)
X_FAR = (0, 1, 2, 3, 4)
Z_FAR, A_FAR = (0, 0)
VIA = ()
STEPS = (
    ((COPY,), (), ((BZ, 1, 1), (BZ, -1, 1), (BX, 1, 0), (BX, -1, 0), (BX2, 2, 0), (AX, 1), (AX, -1), (AX, 2), (AZ, 1, 0, 1), (AZ, -1, 0, 1))),
    ((DQ, 0), (), ()),
    ((DQ, 1), (), ()),
    ((DQ, 2), (), ()),
    ((DQ, 3), (), ()),
    ((DQ, 4), (), ()),
    ((DQ, 5), (), ()),
    ((DQ, 6), (), ()),
    ((DQ, 7), (), ()),
    ((COPY,), ((BZ, -1, 1),), ((BZ, -1, 2),)),
    ((COPY,), ((BZ, 1, 1),), ((BX, 1, 1), (BX, -1, 1), (BX2, 2, 1))),
    ((COPY,), (), ((BZ, 1, 2),)),
    ((DQ, 8), (), ()),
    ((COPY,), ((AZ, 1, 0, 1),), ((AZ, 1, 0, 2),)),
    ((DQ, 9), (), ()),
    ((COPY,), ((AZ, -1, 0, 1),), ((AZ, -1, 0, 2),)),
    ((COPY,), ((AX, 1), (AX, -1)), ((AZ, 1, 1, 1), (AZ, -1, 1, 1))),
    ((COPY,), ((BX, 1, 0), (BX, -1, 0), (BX2, 2, 0)), ((SHB, 0),)),
    ((COPY,), ((AX, 2),), ((SHA, 0),)),
    ((COPY,), (), ((AZ, 1, 2, 1), (AZ, -1, 2, 1))),
    ((MMA, 0, 0), (), ()),
    ((MMA, 0, 1), (), ()),
    ((MMA, 0, 2), (), ()),
    ((COPY,), ((BZ, -1, 2),), ((BZ, -1, 3),)),
    ((MMA, 0, 3), (), ()),
    ((COPY,), ((BZ, 1, 2),), ((BX, 1, 2), (BX, -1, 2), (BX2, 2, 2))),
    ((COPY,), (), ((BZ, 1, 3),)),
    ((MMA, 0, 4), (), ()),
    ((SETTLE, 5), (), ()),
    ((COPY,), ((AZ, 1, 0, 2),), ((AZ, 1, 0, 3),)),
    ((COPY,), ((AZ, -1, 0, 2),), ((AZ, -1, 0, 3),)),
    ((SETTLE, 5), (), ()),
    ((COPY,), ((BX, 1, 1), (BX, -1, 1), (BX2, 2, 1)), ((SHB, 1),)),
    ((COPY,), ((AZ, 1, 1, 1),), ((AZ, 1, 1, 2),)),
    ((COPY,), ((AZ, -1, 1, 1),), ((AZ, -1, 1, 2),)),
    ((MMB, 0, 0), ((SHA, 0), (SHB, 0)), ()),
    ((MMB, 0, 1), (), ()),
    ((MMB, 0, 2), (), ()),
    ((MMB, 0, 3), (), ()),
    ((MMB, 0, 4), (), ()),
    ((SCATTER, 0), (), ((PART, 2, 0), (PART, 1, 0), (PART, -1, 0))),
    ((COPY,), ((AZ, 1, 2, 1), (AZ, -1, 2, 1)), ((SHA, 1),)),
    ((COPY,), (), ((AZ, 1, 2, 2),)),
    ((COPY,), (), ((AZ, -1, 2, 2),)),
    ((TOT, 0), (), ()),
    ((COPY,), ((BZ, 1, 3), (BZ, -1, 3)), ((BX, 1, 3), (BX, -1, 3), (BX2, 2, 3))),
    ((COPY,), (), ((BZ4, 1),)),
    ((COPY,), (), ((BZ4, -1),)),
    ((MMA, 1, 0), (), ()),
    ((MMA, 1, 1), (), ()),
    ((MMA, 1, 2), (), ()),
    ((COPY,), ((AZ, 1, 0, 3),), ((AZ4, 1, 0),)),
    ((COPY,), ((AZ, -1, 0, 3),), ((AZ4, -1, 0),)),
    ((MMA, 1, 3), (), ()),
    ((MMA, 1, 4), (), ()),
    ((COPY,), ((BX, 1, 2), (BX, -1, 2), (BX2, 2, 2)), ((SHB, 2),)),
    ((SETTLE, 13), (), ()),
    ((COPY,), ((AZ, 1, 1, 2),), ((AZ, 1, 1, 3),)),
    ((COPY,), ((AZ, -1, 1, 2),), ((AZ, -1, 1, 3),)),
    ((SETTLE, 5), (), ()),
    ((COPY,), ((AZ, 1, 2, 2),), ((AZ, 1, 2, 3),)),
    ((COPY,), ((AZ, -1, 2, 2),), ((AZ, -1, 2, 3),)),
    ((COPY,), (), ((SHA, 2),)),
    ((MMA, 2, 0), (), ()),
    ((MMB, 1, 0), ((SHA, 1), (SHB, 1)), ()),
    ((MMB, 1, 1), (), ()),
    ((MMB, 1, 2), (), ()),
    ((MMB, 1, 3), (), ()),
    ((MMB, 1, 4), (), ()),
    ((SCATTER, 1), (), ((PART, 2, 1), (PART, 1, 1), (PART, -1, 1))),
    ((MMA, 2, 1), (), ()),
    ((COPY,), ((BZ4, 1), (BZ4, -1)), ((BX, 1, 4), (BX, -1, 4), (BX2, 2, 4))),
    ((MMA, 2, 2), (), ()),
    ((MMA, 2, 3), (), ()),
    ((COPY,), ((BX, 1, 3), (BX, -1, 3), (BX2, 2, 3)), ((SHB, 3),)),
    ((TOT, 1), (), ()),
    ((COLLECT, 0), ((PART, 1, 0), (PART, -1, 0), (PART, 2, 0)), ()),
    ((MMA, 2, 4), (), ()),
    ((COPY,), ((AZ, 1, 1, 3),), ((AZ4, 1, 1),)),
    ((COPY,), ((AZ, -1, 1, 3),), ((AZ4, -1, 1),)),
    ((SETTLE, 12), (), ()),
    ((COPY,), ((AZ, 1, 2, 3),), ((AZ4, 1, 2),)),
    ((COPY,), ((AZ, -1, 2, 3),), ((AZ4, -1, 2),)),
    ((COPY,), (), ((SHA, 3),)),
    ((MMB, 2, 0), ((SHA, 2), (SHB, 2)), ()),
    ((MMB, 2, 1), (), ()),
    ((MMB, 2, 2), (), ()),
    ((MMB, 2, 3), (), ()),
    ((MMB, 2, 4), (), ()),
    ((SCATTER, 2), (), ((PART, 2, 2), (PART, 1, 2), (PART, -1, 2))),
    ((MMA, 3, 0), (), ()),
    ((MMA, 3, 1), (), ()),
    ((TOT, 2), (), ()),
    ((MMA, 3, 2), (), ()),
    ((COPY,), ((BX, 1, 4), (BX, -1, 4), (BX2, 2, 4)), ((SHB, 4),)),
    ((MMA, 3, 3), (), ()),
    ((MMA, 3, 4), (), ()),
    ((COPY,), ((AZ4, 1, 0), (AZ4, -1, 0), (AZ4, 1, 1), (AZ4, -1, 1), (AZ4, 1, 2), (AZ4, -1, 2)), ((SHA, 4),)),
    ((MMA, 4, 0), (), ()),
    ((MMA, 4, 1), (), ()),
    ((MMA, 4, 2), (), ()),
    ((MMA, 4, 3), (), ()),
    ((MMA, 4, 4), (), ()),
    ((COLLECT, 1), ((PART, 1, 1), (PART, -1, 1), (PART, 2, 1)), ()),
    ((MMB, 3, 0), ((SHA, 3), (SHB, 3)), ()),
    ((MMB, 3, 1), (), ()),
    ((MMB, 3, 2), (), ()),
    ((MMB, 3, 3), (), ()),
    ((MMB, 3, 4), (), ()),
    ((SCATTER, 3), (), ((PART, 2, 3), (PART, 1, 3), (PART, -1, 3))),
    ((TOT, 3), (), ()),
    ((SETTLE, 10), (), ()),
    ((MMB, 4, 0), ((SHA, 4), (SHB, 4)), ()),
    ((MMB, 4, 1), (), ()),
    ((MMB, 4, 2), (), ()),
    ((MMB, 4, 3), (), ()),
    ((MMB, 4, 4), (), ()),
    ((SCATTER, 4), (), ((PART, 2, 4), (PART, 1, 4), (PART, -1, 4))),
    ((TOT, 4), (), ((TOT, 1), (TOT, -1), (TOT, 2))),
    ((SETTLE, 8), (), ()),
    ((COLLECT, 2), ((PART, 1, 2), (PART, -1, 2), (PART, 2, 2)), ()),
    ((SETTLE, 14), (), ()),
    ((COLLECT, 3), ((PART, 1, 3), (PART, -1, 3), (PART, 2, 3)), ()),
    ((SETTLE, 6), (), ()),
    ((COLLECT, 4), ((PART, 1, 4), (PART, -1, 4), (PART, 2, 4)), ()),
)


def split(v):
    hi = v.astype(bf16)
    return hi, (v - hi.astype(f32)).astype(bf16)


def dot3(a, b, dims):
    (ah, al), (bh, bl) = a, b

    def one(u, v):
        return lax.dot_general(u, v, (dims, ((), ())), preferred_element_type=f32)

    out = one(ah, bh) + one(ah, bl)
    return out if al is None else out + one(al, bh)


def precondition(q_ref, bo_ref, bi_ref, eig_ref, bd, mid, out):
    bi = bi_ref[...]
    bd[...] = jnp.zeros((128, 128), f32)
    bd[0:64, 0:64] = bi
    bd[64:128, 64:128] = bi
    even, odd = bo_ref[pl.ds(0, 32, stride=2), :], bo_ref[pl.ds(1, 32, stride=2), :]
    q = q_ref[...]
    rows = jnp.concatenate(
        [q[:, b * BLOCK : (b + 1) * BLOCK].astype(f32) for b in range(BLOCKS)], axis=0
    ).astype(bf16)
    bds = split(bd[...])
    mid[...] = dot3((rows, None), bds, ((1,), (0,)))
    t1 = jnp.concatenate([mid[pl.ds(n, BLOCKS, stride=QDEV), :] for n in range(QDEV)], axis=1)
    y = dot3(split(jnp.concatenate([even, odd], axis=1).T), split(t1), ((1,), (0,)))
    low = lax.broadcasted_iota(jnp.int32, (64, 128), 1) < 64
    eig = jnp.concatenate([eig_ref[...], eig_ref[...]], axis=1)
    parts = []
    for n in range(QDEV):
        lanes = slice(n * 128, (n + 1) * 128)
        s = jnp.where(low, y[0:64, lanes], y[64:128, lanes])
        parts.append((s + pltpu.roll(s, 64, 1)) / eig)
    u = jnp.concatenate(parts, axis=1)
    v = dot3(split(jnp.concatenate([even, odd], axis=0)), split(u), ((1,), (0,)))
    low32 = lax.broadcasted_iota(jnp.int32, (32, 128), 1) < 64
    for n in range(QDEV):
        lanes = slice(n * 128, (n + 1) * 128)
        mid[pl.ds(n, BLOCKS, stride=QDEV), :] = jnp.where(low32, v[0:32, lanes], v[32:64, lanes])
    o = dot3(split(mid[...]), bds, ((1,), (1,)))
    for b in range(BLOCKS):
        out[:, b * BLOCK : (b + 1) * BLOCK] = o[QDEV * b : QDEV * (b + 1)]


def kernel(
    q_hbm, mant_hbm, exps_hbm, bo_hbm, bi_hbm, eig_hbm, asg_hbm,
    scores_ref, totals_ref,
    q_ref, exps_ref, bo_ref, bi_ref, eig_ref, asg_ref,
    mant, w, p, acc, fac, mask, bd, mid, prep, xch,
    part_out, part_in, sums, tot, tot_in,
    ss, rs, ls, ms,
):
    e, y = lax.axis_index("ex"), lax.axis_index("lay")
    x, z, c = e // 16, (e // 2) % NZ, e % 2

    def at_x(d):
        return {"ex": (((x + d + NX) % NX) * NZ + z) * 2 + c}

    def at_z(d):
        return {"ex": (x * NZ + (z + d + NZ) % NZ) * 2 + c}

    def at_y(d):
        return {"lay": (y + d + NY) % NY}

    sibling = {"ex": (x * NZ + z) * 2 + 1 - c}

    small = [
        pltpu.make_async_copy(a, b, ls.at[i])
        for i, (a, b) in enumerate(
            (
                (q_hbm, q_ref), (bo_hbm, bo_ref), (bi_hbm, bi_ref),
                (eig_hbm, eig_ref), (exps_hbm, exps_ref), (asg_hbm, asg_ref),
            )
        )
    ]
    for cp in small:
        cp.start()
    loads = [
        pltpu.make_async_copy(
            mant_hbm.at[pl.ds(i * TCH, TCH)], mant.at[pl.ds(i * TCH, TCH)], ms.at[i]
        )
        for i in range(NCH)
    ]
    barrier = pltpu.get_barrier_semaphore()
    partners = [at_x(d) for d in (1, -1, 2)] + [at_y(d) for d in (1, -1, 2)]
    steps = {1} | {k for k in (2, 3) if k not in Z_STEP or k not in A_STEP}
    partners += [at_z(d * k) for k in sorted(steps) for d in (1, -1)] + [sibling]
    if Z_FAR or A_FAR:
        partners.append(at_z(4))
    for dev in partners:
        pl.semaphore_signal(barrier, inc=1, device_id=dev, device_id_type=MESH)
    for cp in loads:
        cp.start()

    copies, live = {}, []

    def remote(name, src, dst, dev):
        i = len(copies)
        copies[name] = pltpu.make_async_remote_copy(
            src_ref=src, dst_ref=dst, send_sem=ss.at[i], recv_sem=rs.at[i],
            device_id=dev, device_id_type=MESH,
        )

    def send(*name):
        copies[name].start()
        live.append(name)

    def arrived(*name):
        copies[name].wait_recv()

    def settle(keep=0):
        while len(live) > keep:
            copies[live.pop(0)].wait_send()

    def lanes(first, count):
        return pl.ds(pl.multiple_of(c * HALF + first, 128), count)

    la, lb, lhalf = lanes(0, KA), lanes(KA, KB), lanes(0, HALF)
    for d in (1, -1):
        hi = 0 if d == 1 else 1
        la2 = lanes(hi * (KA // 2), KA // 2)
        lb2 = lanes(KA + hi * (KB // 2), KB // 2)
        hops = [ZSLOT[(-d * k) % NZ] for k in (0, 1, 2, 3)]
        for k in (1, 2, 3):
            via = k - 1 if k in Z_STEP else 0
            remote(
                (BZ, d, k), p.at[hops[via], 0, :, lb], p.at[hops[k], 0, :, lb], at_z(d * (k - via))
            )
        if not Z_FAR:
            remote((BZ4, d), p.at[hops[3], 0, :, lb2], p.at[ZSLOT[4], 0, :, lb2], at_z(d))
        elif d == 1:
            remote((BZ4, 2), p.at[0, 0, :, lb], p.at[ZSLOT[4], 0, :, lb], at_z(4))
        for i, (first, count) in enumerate(XBLK):
            blk = pl.ds(first, count)
            for k in (1, 2, 3):
                via = k - 1 if k in A_STEP else 0
                remote(
                    (AZ, d, i, k),
                    p.at[hops[via], blk, :, la], p.at[hops[k], blk, :, la], at_z(d * (k - via)),
                )
            if not A_FAR:
                remote(
                    (AZ4, d, i), p.at[hops[3], blk, :, la2], p.at[ZSLOT[4], blk, :, la2], at_z(d)
                )
            elif d == 1:
                remote((AZ4, 2, i), p.at[0, blk, :, la], p.at[ZSLOT[4], blk, :, la], at_z(4))
        near = XSLOT[(-d) % NX]
        for i, (first, count) in enumerate(DIST):
            blk = pl.ds(first, count)
            remote((BX, d, i), p.at[blk, 0, :, lb], p.at[blk, near, :, lb], at_x(d))
            if i not in X_FAR:
                remote((BX2, d, i), p.at[blk, near, :, lb2], p.at[blk, 3, :, lb2], at_x(d))
            elif d == 1:
                remote((BX2, 2, i), p.at[blk, 0, :, lb], p.at[blk, 3, :, lb], at_x(2))
        remote((AX, d), p.at[0, 0, :, la], p.at[0, near, :, la], at_x(d))
    remote((AX, 2), p.at[0, 0, :, la], p.at[0, 3, :, la], at_x(2))
    for g, (first, count) in enumerate(GROUP):
        blk = pl.ds(first, count)
        remote((SHA, g), p.at[blk, :, :, la], p.at[blk, :, :, la], sibling)
        remote((SHB, g), p.at[blk, :, :, lb], p.at[blk, :, :, lb], sibling)
        if g in VIA:
            for i, d in enumerate((1, -1)):
                t = pl.ds(i * HT, HT)
                remote(
                    (Y2, d, g), part_out.at[2, blk, :, t], part_in.at[2, blk, :, t], at_y(d)
                )
                remote((Y1, d, g), part_out.at[i, blk], part_in.at[i, blk], at_y(d))
        else:
            for i, d in enumerate((1, -1, 2)):
                remote((PART, d, g), part_out.at[i, blk], part_in.at[i, blk], at_y(d))
    for i, d in enumerate((1, -1, 2)):
        remote((TOT, d), tot, tot_in.at[i], at_y(d))
    other_cols = pl.ds(pl.multiple_of((1 - c) * HALF, HALF), HALF)
    own_cols = pl.ds(pl.multiple_of(c * HALF, HALF), HALF)
    remote((SWAP,), prep.at[:, other_cols], xch.at[c], sibling)

    for cp in small[:4]:
        cp.wait()
    precondition(q_ref, bo_ref, bi_ref, eig_ref, bd, mid, prep)
    pl.semaphore_wait(barrier, len(partners))
    send(SWAP)
    for cp in small[4:]:
        cp.wait()
    exps = exps_ref[...]
    factor = jnp.zeros(exps.shape, f32)
    for exponent in range(lowest_exponent, highest_exponent):
        factor = factor + jnp.where(exps == exponent, f32(2.0**exponent), f32(0.0))
    fac[...] = factor

    def dequantize(i):
        loads[i].wait()
        t = pl.ds(i * TCH, TCH)
        for b in range(BLOCKS):
            rows = pl.ds(b * BLOCK, BLOCK)
            w[rows, t] = mant[t, rows].T * fac[b : b + 1, t].astype(bf16)

    def multiply(g, n, part):
        first, count = GROUP[g]
        blk = pl.ds(first, count)
        k = pl.ds(pl.multiple_of((c if part == 0 else 1 - c) * HALF, HALF), HALF)
        cols = pl.ds(n * NT, NT)
        rows = count * NX * PAIR
        a = p[blk, :, :, k].reshape(rows, HALF)
        if rows < 128:
            a = jnp.concatenate([a, jnp.zeros((128 - rows, HALF), bf16)], axis=0)
        r = jnp.dot(a, w[k, cols], preferred_element_type=f32)[0:rows]
        r = r.reshape(count, NX, PAIR, NT)
        acc[blk, :, :, cols] = r if part == 0 else acc[blk, :, :, cols] + r

    def slot_of(d):
        xr = (y + d + NY - x + NX) % NX
        return xr + xr // 2 - 2 * (xr // 3)

    def add_totals(g):
        t0, t1 = None, None
        first, count = GROUP[g]
        for s in range(first, first + count):
            zo = (z + ZORDER[s]) % NZ
            for j in range(NX):
                xo = (x + XORDER[j]) % NX
                m = mask[xo, pl.ds(pl.multiple_of(zo * PAIR, PAIR), PAIR), :]
                m = jnp.concatenate([m] * (ROWS // 128), axis=1)
                v = acc[s, j]
                p1 = v * m
                p0 = v - p1
                p0, p1 = p0[0:8] + p0[8:16], p1[0:8] + p1[8:16]
                t0, t1 = (p0, p1) if t0 is None else (t0 + p0, t1 + p1)
        for i, t in enumerate((t0, t1)):
            sums[i] = t if g == 0 else sums[i] + t
        if g == len(GROUP) - 1:
            tot[...] = jnp.zeros(tot.shape, f32)
            for i in range(2):
                total = jnp.sum(sums[i], axis=0, keepdims=True)
                for n in range(ROWS // NT):
                    tot[8 * i + n : 8 * i + n + 1, :] = total[:, n * NT : (n + 1) * NT]

    def scatter(g):
        first, count = GROUP[g]
        for i, d in ((2, 2),) if g in VIA else ((2, 2), (0, 1), (1, -1)):
            to = slot_of(d)
            for s in range(first, first + count):
                part_out[i, s] = acc[s, to].astype(bf16)

    def combine(g):
        first, count = GROUP[g]
        for i, d in ((0, 1), (1, -1)):
            to = slot_of(d)
            for j in range(2):
                t = pl.ds(j * HT, HT)
                for s in range(first, first + count):
                    v = acc[s, to, :, t]
                    v = v + part_in[2, s, :, t].astype(f32) if i == j else v
                    part_out[i, s, :, t] = v.astype(bf16)

    normalizer = 1.0 / math.sqrt(NY * ENTRIES)

    def collect(g):
        mine = slot_of(0)
        first, count = GROUP[g]
        for s in range(first, first + count):
            total = acc[s, mine] + part_in[0, s].astype(f32)
            total = total + part_in[1, s].astype(f32)
            if g not in VIA:
                total = total + part_in[2, s].astype(f32)
            zo = (z + ZORDER[s]) % NZ
            scores_ref[pl.ds(pl.multiple_of(zo * PAIR, PAIR), PAIR), :] = total * normalizer

    do = {
        COPY: lambda: None, SETTLE: lambda n: settle(max(len(live) - n, 0)),
        DQ: lambda i: None if i < EARLY else dequantize(i),
        MMA: lambda g, n: multiply(g, n, 0), MMB: lambda g, n: multiply(g, n, 1),
        SCATTER: scatter, COMB: combine, TOT: add_totals, COLLECT: collect,
    }
    xch[c] = prep[:, own_cols]
    for i in range(EARLY):
        dequantize(i)
    arrived(SWAP)
    p[0, 0, :, lhalf] = xch[...].reshape(PAIR, HALF).astype(bf16)
    for i, ((step, *args), waits, sends) in enumerate(STEPS):
        if i == 1:
            for j in range(NX):
                one = (asg_ref[:, j * 128 : (j + 1) * 128] == 1).astype(f32)
                mask[j] = jnp.broadcast_to(one, (128, 128)).T
        if i == len(STEPS) - 1:
            settle(6)
        for name in waits:
            arrived(*name)
        do[step](*args)
        for name in sends:
            send(*name)
    for d in (1, -1, 2):
        arrived(TOT, d)
    total = tot[...] + tot_in[0] + tot_in[1] + tot_in[2]
    for i in range(2):
        for n in range(ROWS // NT):
            row = total[8 * i + n : 8 * i + n + 1, :]
            totals_ref[i : i + 1, n * NT : (n + 1) * NT] = row * (normalizer / math.sqrt(QB))
    settle()


N_COPIES = 2 * (3 + 1 + 4 * len(XBLK) + 10 + 1) - len(X_FAR) - Z_FAR - A_FAR * len(XBLK) + 1 + 5 * len(GROUP) + len(VIA) + 3 + 1


def body(queries, train_mantissa, scale_exponents, basis_out, basis_in, eigen, assignment):
    hbm = pl.BlockSpec(memory_space=pl.ANY)
    vmem = pltpu.VMEM
    dma = pltpu.SemaphoreType.DMA
    piece = (3, NZ, PAIR, ROWS)
    scores, totals = pl.pallas_call(
        kernel,
        out_shape=(
            pltpu.VMEM((NX * 32, ROWS), f32),
            pltpu.VMEM((2, ROWS), f32),
        ),
        in_specs=[hbm] * 7,
        out_specs=(pl.BlockSpec(memory_space=pltpu.VMEM),) * 2,
        scratch_shapes=[
            vmem((QDEV, ENTRIES), bf16),
            vmem((BLOCKS, ROWS), jnp.int32),
            vmem((ORDER, ORDER), f32),
            vmem((ORDER, ORDER), f32),
            vmem((ORDER, ORDER), f32),
            vmem((1, 512), jnp.int32),
            vmem((ROWS, ENTRIES), bf16),
            vmem((ENTRIES, ROWS), bf16),
            vmem((NZ, NX, PAIR, ENTRIES), bf16),
            vmem((NZ, NX, PAIR, ROWS), f32),
            vmem((BLOCKS, ROWS), f32),
            vmem((NX, 128, 128), f32),
            vmem((128, 128), f32),
            vmem((BLOCKS * QDEV, 128), f32),
            vmem((QDEV, ENTRIES), f32),
            vmem((2, QDEV, HALF), f32),
            vmem(piece, bf16),
            vmem(piece, bf16),
            vmem((2, 8, ROWS), f32),
            vmem((16, NT), f32),
            vmem((3, 16, NT), f32),
            dma((N_COPIES,)),
            dma((N_COPIES,)),
            dma((6,)),
            dma((NCH,)),
        ],
        compiler_params=pltpu.CompilerParams(
            collective_id=0, has_side_effects=True, vmem_limit_bytes=56 * 2**20
        ),
        name="influence",
    )(
        queries.reshape(QDEV, ENTRIES),
        train_mantissa.reshape(ROWS, ENTRIES),
        scale_exponents.reshape(ROWS, BLOCKS).T,
        basis_out.reshape(ORDER, ORDER),
        basis_in.reshape(ORDER, ORDER),
        eigen.reshape(ORDER, ORDER),
        assignment.reshape(1, 512),
    )
    return scores, totals


def solution(mesh):
    placed = (
        P("ex", "lay", None),
        P("ex", "lay", None),
        P("ex", "lay", None),
        P("lay", None, None),
        P("lay", None, None),
        P("lay", None, None),
        P(),
    )
    return jax.shard_map(
        body, mesh=mesh, in_specs=placed, out_specs=(P("lay", "ex"), P(None, "ex")), check_vma=False
    )
```
